32 devices in a mesh: wide: 4 (over y, core), narrow: 8 (over z, x).
Axes of the slice: x: 2, y: 2, z: 4, core: 2. Of those that a mesh axis runs over, the one named last changes fastest.
Arguments:
- loads: float32 [128, 24, 128], P(('wide', 'narrow')), may hold values from -6 to 6
- diagonal: float32 [128, 128], P(('wide', 'narrow')), may hold values from 2 to 7
- stiffness: float32 [128, 4, 128, 128], P(('wide', 'narrow')), may hold values from 0 to 0.001953125
- neighbors: int32 [128, 4], P(('wide', 'narrow')), may hold values from 0 to 7
- slot_mask: int32 [128, 4], P(('wide', 'narrow')), may hold values 0 or 1
- send_list: int32 [128], P(('wide', 'narrow')), may hold values from 0 to 3
- aggregate: int32 [128, 128], P(('wide', 'narrow')), may hold values from 0 to 127
- coarse_inverse: float32 [512, 512], P(('wide', 'narrow')), may hold values from -0.03125 to 0.03125
Outputs:
- correction: float32 [128, 24, 128], P(('wide', 'narrow'))
- residual: float32 [128, 24, 128], P(('wide', 'narrow'))
The draws below stay inside these ranges and needn't reach their ends.
Inputs may be any that keep to these rules, and one draw needn't show every extreme that they name: `neighbors`: indices into the extended list of the block's group. `send_list`: block indices within the sending group. aggregate indices among the 128 aggregates of the particle's wide coordinate.
All inputs are finite; a program needn't handle non-finite values. No bound on the sum of `slot_mask` on one device may be relied on, other than what follows from the above.
Results may differ from the reference program's by a relative error of at most 0.00025.
Values sent between devices are 32-bit elements; how exact they have to be, the bound alone decides.
No kernel may reach another device: no remote copies, remote signals or barrier semaphores. Data moves between devices by JAX's collectives and lax.ppermute only.
A program may use at most 64 MiB of HBM per device.

```python
import jax
import jax.numpy as jnp
from jax import lax

BS = 128
NB = 4
NS = 4
SWEEPS = 2
AGG_DEV = 16
GHOST = 2
VEC = 24
BLOCKS = 128
SENDS = 128
AGG_W = 128
NC = 512
N_WIDE = 4
N_NARROW = 8


def draw_diagonal(key, part):
    count = BLOCKS * BS
    place = jnp.arange(count, dtype=jnp.float32).reshape(BLOCKS, BS) / max(count - 1, 1)
    level = 3.0 - 2.0 * place
    spread = jax.random.uniform(key, (BLOCKS, BS), jnp.float32)
    return (1.0 + level * (1.0 + spread)).astype(jnp.float32)


def plant(array, stream_key, smallest, top_value):
    spot = [jax.random.randint(jax.random.fold_in(stream_key, axis), (), 0, length) for axis, length in enumerate(array.shape)]
    widest = array.shape.index(max(array.shape))
    beside = spot[:widest] + [(spot[widest] + 1) % array.shape[widest]] + spot[widest + 1:]
    return array.at[tuple(spot)].set(smallest).at[tuple(beside)].set(top_value)


def shard_levels(own_key, dims, shards, least, high):
    gain = 1.0
    for axis_at, shards_of in shards:
        draws = jax.random.uniform(jax.random.fold_in(jax.random.fold_in(own_key, 6), axis_at), (shards_of,), jnp.float32, least / len(shards), high / len(shards))
        gain = gain * jnp.repeat(jnp.exp(draws), dims[axis_at] // shards_of).reshape((-1,) + (1,) * (len(dims) - 1 - axis_at))
    return gain


def gaussian(stream_key, dims, deviation, limit, cuts=(), kind=jnp.bfloat16):
    array = deviation * jax.random.normal(stream_key, dims, jnp.float32)
    if cuts:
        array = array * shard_levels(stream_key, dims, cuts, -0.22, 0.18)
    return jnp.clip(array, -limit, limit).astype(kind)


def setup_inputs(seed: int = 0) -> dict:
    keys = jax.random.split(jax.random.key(seed), 9)
    return {
        "loads": gaussian(keys[0], (BLOCKS, VEC, BS), 1.0, 6.0, ((0, 32),), jnp.float32),
        "diagonal": draw_diagonal(jax.random.fold_in(keys[8], 71), 0),
        "stiffness": jnp.clip(0.001953125 * jax.random.uniform(keys[2], (BLOCKS, NS, BS, BS), jnp.float32) ** shard_levels(keys[2], (BLOCKS, NS, BS, BS), ((0, 32),), -0.2, 0.2), 0.0, 0.001953125),
        "neighbors": plant(jax.random.randint(keys[3], (BLOCKS, NS), 0, NB + 2 * GHOST), jax.random.fold_in(keys[3], 1), 0, (NB + 2 * GHOST) - 1).astype(jnp.int32),
        "slot_mask": plant((jax.random.randint(keys[4], (BLOCKS, NS), 0, 4) < 3).astype(jnp.int32), jax.random.fold_in(keys[4], 1), 0, 1),
        "send_list": plant(jax.random.randint(keys[5], (SENDS,), 0, NB), jax.random.fold_in(keys[5], 1), 0, NB - 1).astype(jnp.int32),
        "aggregate": plant(jax.random.randint(keys[6], (BLOCKS, BS), 0, AGG_DEV * N_NARROW), jax.random.fold_in(keys[6], 1), 0, (AGG_DEV * N_NARROW) - 1).astype(jnp.int32),
        "coarse_inverse": gaussian(keys[7], (NC, NC), (NC * 64) ** -0.5, 0.03125, ((0, 32),), jnp.float32),
    }


highest = lax.Precision.HIGHEST


def extended_lists(send_list):
    groups = N_WIDE * N_NARROW
    sending = send_list.reshape(groups, 2 * GHOST)
    group_ids = jnp.arange(groups, dtype=jnp.int32)
    wide_ids = group_ids // N_NARROW
    own_blocks = group_ids[:, None] * NB + jnp.arange(NB, dtype=jnp.int32)[None, :]
    left_group = jnp.clip(group_ids - N_NARROW, 0, groups - 1)
    right_group = jnp.clip(group_ids + N_NARROW, 0, groups - 1)
    left_blocks = left_group[:, None] * NB + sending[left_group, GHOST:]
    right_blocks = right_group[:, None] * NB + sending[right_group, :GHOST]
    index_table = jnp.concatenate([own_blocks, left_blocks, right_blocks], axis=1).astype(jnp.int32)
    left_valid = jnp.broadcast_to((wide_ids > 0)[:, None], (groups, GHOST))
    right_valid = jnp.broadcast_to((wide_ids < N_WIDE - 1)[:, None], (groups, GHOST))
    own_valid = jnp.ones((groups, NB), jnp.bool_)
    valid_table = jnp.concatenate([own_valid, left_valid, right_valid], axis=1).astype(jnp.float32)
    return index_table, valid_table


def reference(loads, diagonal, stiffness, neighbors, slot_mask, send_list, aggregate, coarse_inverse):
    groups = N_WIDE * N_NARROW
    index_table, valid_table = extended_lists(send_list)
    grouped = neighbors.reshape(groups, NB * NS).astype(jnp.int32)
    global_nbr = jnp.take_along_axis(index_table, grouped, axis=1).reshape(BLOCKS, NS)
    live_slots = slot_mask.astype(jnp.float32)
    weights_live = jnp.take_along_axis(valid_table, grouped, axis=1).reshape(BLOCKS, NS) * live_slots
    diag_rows = diagonal[:, None, :]

    def operate(vector):
        gathered = vector[global_nbr] * weights_live[:, :, None, None]
        coupled = jnp.einsum("bscj,bsij->bci", gathered, stiffness, precision=highest)
        return diag_rows * vector - coupled

    row_abs = lax.map(lambda block_group: jnp.sum(jnp.abs(block_group), axis=3),
                      stiffness.reshape(groups, NB, NS, BS, BS)).reshape(BLOCKS, NS, BS)
    row_ratio = jnp.sum(row_abs * live_slots[:, :, None], axis=1) / diagonal
    upper_bound = 1.0 + jnp.max(row_ratio)
    centre = 0.625 * upper_bound
    half_span = 0.375 * upper_bound
    spread_ratio = 5.0 / 3.0
    weight_prev = 0.6
    direction = (loads / diag_rows) / centre
    solution = direction
    remainder = loads
    for sweep_index in range(SWEEPS):
        remainder = remainder - operate(direction)
        weight_now = 1.0 / (2.0 * spread_ratio - weight_prev)
        direction = (weight_now * weight_prev) * direction + ((2.0 * weight_now / half_span) * remainder) / diag_rows
        solution = solution + direction
        weight_prev = weight_now
    residual = remainder - operate(direction)
    wide_of_block = jnp.arange(BLOCKS, dtype=jnp.int32) // (NB * N_NARROW)
    global_agg = (wide_of_block[:, None] * AGG_W + aggregate).astype(jnp.int32)
    flat_res = jnp.transpose(residual, (0, 2, 1)).reshape(BLOCKS * BS, VEC)
    coarse_rhs = jax.ops.segment_sum(flat_res, global_agg.reshape(-1), num_segments=NC)
    coarse_sol = jnp.dot(coarse_inverse, coarse_rhs, precision=highest, preferred_element_type=jnp.float32)
    spread_back = jnp.transpose(coarse_sol[global_agg], (0, 2, 1))
    return solution + spread_back, residual
```

```python
import functools

import jax
import jax.numpy as jnp
from jax import lax
from jax.experimental import pallas as pl
from jax.experimental.pallas import tpu as pltpu
from jax.sharding import PartitionSpec as P

SWEEPS = 2
AXES = ("wide", "narrow")

VMEM = pl.BlockSpec(memory_space=pltpu.VMEM)
SMEM = pl.BlockSpec(memory_space=pltpu.SMEM)
LIMIT = pltpu.CompilerParams(vmem_limit_bytes=32 * 1024 * 1024)

f32 = jnp.float32
bf16 = jnp.bfloat16
TRANSPOSED = (((1,), (1,)), ((), ()))


def like(*shape, dtype=f32):
    return jax.ShapeDtypeStruct(shape, dtype)


def split(value):
    high = value.astype(bf16).astype(f32)
    return high, value - high


def parity():
    return lax.rem(lax.axis_index("wide"), 2)


def write_messages(send_ref, field_ref, near_ref, far_ref):
    odd = parity()
    ghosts = near_ref.shape[0]
    for j in range(ghosts):
        near_ref[j] = field_ref[send_ref[(1 - odd) * ghosts + j]]
        far_ref[j] = field_ref[send_ref[odd * ghosts + j]]


def start_kernel(send_ref, loads_ref, diagonal_ref, field_ref, near_ref, far_ref):
    for b in range(loads_ref.shape[0]):
        field_ref[b] = loads_ref[b] / diagonal_ref[b : b + 1, :]
    write_messages(send_ref, field_ref, near_ref, far_ref)


def prepare_kernel(mask_ref, stiffness_ref, diagonal_ref, parts_ref, peak_ref):
    blocks, slots, size, _ = stiffness_ref.shape
    peak = jnp.zeros((8, size), f32)
    for b in range(blocks):
        total = jnp.zeros((size, size), f32)
        for s in range(slots):
            live = stiffness_ref[b, s] * mask_ref[b, s].astype(f32)
            high, low = split(live)
            parts_ref[b, 0:size, s * size : (s + 1) * size] = high.astype(bf16)
            parts_ref[b, size : 2 * size, s * size : (s + 1) * size] = low.astype(bf16)
            total = total + jnp.abs(live)
        rows = lax.dot_general(
            jnp.ones((8, size), f32), total, TRANSPOSED,
            precision=lax.Precision.HIGHEST, preferred_element_type=f32,
        )
        peak = jnp.maximum(peak, rows / diagonal_ref[b : b + 1, :])
    peak_ref[...] = jnp.broadcast_to(jnp.max(peak, axis=1, keepdims=True), peak.shape)


def couple(neighbors_ref, field_ref, near_ref, far_ref, parts_ref, extended_ref, b_out):
    blocks, comps, size = field_ref.shape
    slots = neighbors_ref.shape[1]
    ghosts = near_ref.shape[0]
    wide = lax.axis_size("wide")
    me = lax.axis_index("wide")
    odd = parity()
    inside = jnp.where((me == 0) | (me == wide - 1), 0.0, 1.0).astype(f32)

    def put(place, value):
        extended_ref[place] = jnp.concatenate(split(value), axis=0).astype(bf16)

    for b in range(blocks):
        put(b, field_ref[b])
    for j in range(ghosts):
        put(blocks + j, near_ref[j])
        put(blocks + ghosts + j, far_ref[j] * inside)
    for b in range(blocks):
        rows = []
        for s in range(slots):
            entry = neighbors_ref[b, s]
            lower = entry < blocks + ghosts
            swapped = jnp.where(lower, entry + ghosts, entry - ghosts)
            entry = jnp.where((entry >= blocks) & (odd == 0), swapped, entry)
            rows.append(extended_ref[entry])
        product = lax.dot_general(
            jnp.concatenate(rows, axis=1), parts_ref[b], TRANSPOSED, preferred_element_type=f32
        )
        b_out(b, product[:comps, :size] + product[:comps, size:] + product[comps:, :size])


def step_kernel(
    neighbors_ref, send_ref, field_ref, near_ref, far_ref, parts_ref, diagonal_ref,
    next_ref, near_out, far_out, extended_ref,
):
    def put(b, coupled):
        next_ref[b] = coupled / diagonal_ref[b : b + 1, :]

    couple(neighbors_ref, field_ref, near_ref, far_ref, parts_ref, extended_ref, put)
    write_messages(send_ref, next_ref, near_out, far_out)


def coefficients(upper):
    half_span = 0.375 * upper
    zero = jnp.zeros_like(upper)
    ratio = 5.0 / 3.0
    before = 0.6

    def applied(d):
        return [d[0]] + [d[k] - d[k - 1] for k in range(1, len(d))] + [-d[-1]]

    def less(a, b):
        a = a + [zero] * (len(b) - len(a))
        return [x - y for x, y in zip(a, b)]

    direction = [1.0 / (0.625 * upper)]
    answer = list(direction)
    remainder = [jnp.ones_like(upper)]
    for _ in range(SWEEPS):
        remainder = less(remainder, applied(direction))
        now = 1.0 / (2.0 * ratio - before)
        longer = direction + [zero]
        direction = [now * before * d + (2.0 * now / half_span) * r for d, r in zip(longer, remainder)]
        answer = [a + d for a, d in zip(answer + [zero], direction)]
        before = now
    return less(remainder, applied(direction)), answer


def last_kernel(
    neighbors_ref, field0_ref, field1_ref, field2_ref, near_ref, far_ref, parts_ref, diagonal_ref, peak_ref, aggregate_ref,
    residual_ref, answer_ref, sums_ref, extended_ref,
):
    blocks, comps, size = field0_ref.shape
    members = sums_ref.shape[1]
    on_residual, on_answer = coefficients(1.0 + peak_ref[0:1, :])

    def put(b, coupled):
        scale = diagonal_ref[b : b + 1, :]
        fields = [field0_ref[b], field1_ref[b], field2_ref[b], coupled / scale]
        residual_ref[b] = scale * sum(c * f for c, f in zip(on_residual, fields))
        answer_ref[b] = sum(c * f for c, f in zip(on_answer, fields))

    couple(neighbors_ref, field2_ref, near_ref, far_ref, parts_ref, extended_ref, put)
    index = lax.broadcasted_iota(jnp.int32, (members, size), 0)
    values, places = [], []
    for b in range(blocks):
        values.append(jnp.concatenate(split(residual_ref[b]), axis=0).astype(bf16))
        places.append((index == aggregate_ref[b : b + 1, :]).astype(f32).astype(bf16))
    product = lax.dot_general(
        jnp.concatenate(values, axis=1), jnp.concatenate(places, axis=1), TRANSPOSED, preferred_element_type=f32
    )
    sums_ref[...] = product[:comps] + product[comps:]


def coarse_kernel(own_ref, other_ref, inverse_ref, aggregate_ref, answer_ref, correction_ref):
    blocks, comps, size = answer_ref.shape
    members, unknowns = inverse_ref.shape
    odd = parity()
    rank = lax.axis_index("narrow")
    rows_each = members // lax.axis_size("narrow")
    own, other = own_ref[...], other_ref[...]
    rhs = jnp.where(odd == 0, jnp.concatenate([own, other], axis=0), jnp.concatenate([other, own], axis=0))
    left = jnp.concatenate(split(rhs), axis=0).astype(bf16)
    right = jnp.concatenate(split(inverse_ref[...]), axis=0).astype(bf16)
    product = lax.dot_general(left, right, TRANSPOSED, preferred_element_type=f32)
    found = product[:comps, :members] + product[:comps, members:] + product[comps:, :members]
    found = jnp.concatenate(split(found), axis=0).astype(bf16)
    index = lax.broadcasted_iota(jnp.int32, (members, size), 0) ^ (rank * rows_each)
    for b in range(blocks):
        place = (index == aggregate_ref[b : b + 1, :]).astype(f32).astype(bf16)
        spread = jnp.dot(found, place, preferred_element_type=f32)
        correction_ref[b] = answer_ref[b] + spread[:comps] + spread[comps:]


def swap(value, axis, bit):
    return lax.ppermute(value, axis, [(i, i ^ bit) for i in range(lax.axis_size(axis))])


def swap_far(value):
    count = lax.axis_size("wide")
    return lax.ppermute(value, "wide", [(i, (i + 1 if i % 2 else i - 1) % count) for i in range(count)])


def bits(axis):
    return [1 << k for k in range(lax.axis_size(axis).bit_length() - 1)]


def shards(loads, diagonal, stiffness, neighbors, slot_mask, send_list, aggregate, coarse_inverse):
    blocks, comps, size = loads.shape
    slots = neighbors.shape[1]
    ghosts = send_list.shape[0] // 2
    wide, narrow = lax.axis_size("wide"), lax.axis_size("narrow")
    members = coarse_inverse.shape[0] * narrow
    field = like(blocks, comps, size)
    message = like(ghosts, comps, size)
    extended = pltpu.VMEM((blocks + 2 * ghosts, 2 * comps, size), bf16)

    def call(kernel, in_specs, out_shape, scratch=()):
        return pl.pallas_call(
            kernel, in_specs=in_specs, out_specs=jax.tree.map(lambda _: VMEM, out_shape), out_shape=out_shape,
            scratch_shapes=scratch, compiler_params=LIMIT,
        )

    field0, near, far = call(start_kernel, [SMEM, VMEM, VMEM], (field, message, message))(send_list, loads, diagonal)
    near, far = swap(near, "wide", 1), swap_far(far)
    parts, peak = call(
        prepare_kernel, [SMEM, VMEM, VMEM],
        (like(blocks, 2 * size, slots * size, dtype=bf16), like(8, size)),
    )(slot_mask, stiffness, diagonal)

    for axis in AXES:
        for bit in bits(axis):
            peak = jnp.maximum(peak, swap(peak, axis, bit))
    inverse = coarse_inverse
    for bit in bits("narrow"):
        inverse = jnp.concatenate([inverse, swap(inverse, "narrow", bit)], axis=0)

    step = call(step_kernel, [SMEM] * 2 + [VMEM] * 5, (field, message, message), [extended])
    field1, near, far = step(neighbors, send_list, field0, near, far, parts, diagonal)
    near, far = swap(near, "wide", 1), swap_far(far)
    field2, near, far = step(neighbors, send_list, field1, near, far, parts, diagonal)
    near, far = swap(near, "wide", 1), swap_far(far)
    residual, answer, sums = call(
        last_kernel, [SMEM] + [VMEM] * 9, (field, field, like(comps, members)), [extended]
    )(neighbors, field0, field1, field2, near, far, parts, diagonal, peak, aggregate)

    half = comps // 2
    quarter = half // 4
    outgoing = jnp.broadcast_to(
        sums.reshape(1, 2, 1, quarter, 4, members), (wide // 2, 2, narrow, quarter, 4, members)
    ).reshape(wide * narrow, quarter, 4, members)
    incoming = lax.all_to_all(outgoing, AXES, 0, 0)
    own = incoming.reshape(wide, narrow, half, members).sum(axis=1)
    own = own.transpose(1, 0, 2).reshape(half, wide * members)
    other = swap(own, "wide", 1)
    correction = call(coarse_kernel, [VMEM] * 5, field)(own, other, inverse, aggregate, answer)
    return correction, residual


def solution(mesh):
    return jax.shard_map(
        shards,
        mesh=mesh,
        in_specs=(
            P(AXES, None, None),
            P(AXES, None),
            P(AXES, None, None, None),
            P(AXES, None),
            P(AXES, None),
            P(AXES),
            P(AXES, None),
            P(AXES, None),
        ),
        out_specs=(P(AXES, None, None), P(AXES, None, None)),
        check_vma=False,
    )
```

```python
import jax
import jax.numpy as jnp
from jax import lax
from jax.experimental import pallas as pl
from jax.experimental.pallas import tpu as pltpu
from jax.sharding import PartitionSpec as P

SWEEPS = 2
AXES = ("wide", "narrow")

VMEM = pl.BlockSpec(memory_space=pltpu.VMEM)
SMEM = pl.BlockSpec(memory_space=pltpu.SMEM)
HBM = pl.BlockSpec(memory_space=pl.ANY)
LIMIT = pltpu.CompilerParams(vmem_limit_bytes=32 * 1024 * 1024)

f32 = jnp.float32
bf16 = jnp.bfloat16
TRANSPOSED = (((1,), (1,)), ((), ()))


def like(*shape, dtype=f32):
    return jax.ShapeDtypeStruct(shape, dtype)


def split(value):
    high = value.astype(bf16).astype(f32)
    return high, value - high


def stacked(value):
    return jnp.concatenate(split(value), axis=0).astype(bf16)


def beside(value):
    return jnp.concatenate(split(value), axis=1).astype(bf16)


def parity():
    return lax.rem(lax.axis_index("wide"), 2)


def write_messages(choice_ref, field_ref, near_ref, far_ref):
    blocks, comps, _ = field_ref.shape
    ghosts = near_ref.shape[0] // comps
    for side, ref in enumerate((near_ref, far_ref)):
        for j in range(ghosts):
            row = (side * ghosts + j) * blocks
            ref[j * comps : (j + 1) * comps] = sum(
                choice_ref[row + b : row + b + 1, :] * field_ref[b] for b in range(blocks)
            )


def start_copies(pairs, sems):
    copies = [pltpu.make_async_copy(source, target, sems.at[k]) for k, (source, target) in enumerate(pairs)]
    for copy in copies:
        copy.start()
    return copies


def start_kernel(
    send_hbm, loads_hbm, diagonal_hbm, stiffness_hbm,
    field_ref, near_ref, far_ref, diagonal_ref, choice_ref, stiffness_ref,
    loads_ref, send_ref, sems,
):
    blocks, _, size = loads_ref.shape
    ghosts = send_ref.shape[0] // 2
    copies = start_copies([
        (send_hbm, send_ref), (diagonal_hbm, diagonal_ref), (loads_hbm, loads_ref), (stiffness_hbm, stiffness_ref)
    ], sems)
    for copy in copies[:3]:
        copy.wait()
    odd = parity()
    for j in range(ghosts):
        for b in range(blocks):
            near = jnp.where(send_ref[(1 - odd) * ghosts + j] == b, 1.0, 0.0)
            far = jnp.where(send_ref[odd * ghosts + j] == b, 1.0, 0.0)
            choice_ref[j * blocks + b : j * blocks + b + 1, :] = jnp.full((1, size), near, f32)
            row = (ghosts + j) * blocks + b
            choice_ref[row : row + 1, :] = jnp.full((1, size), far, f32)
    for b in range(blocks):
        field_ref[b] = loads_ref[b] / diagonal_ref[b : b + 1, :]
    write_messages(choice_ref, field_ref, near_ref, far_ref)
    copies[3].wait()


def prepare_kernel(
    neighbors_hbm, mask_hbm, aggregate_hbm, stiffness_ref, diagonal_ref, parts_ref, places_ref, peak_ref,
    total_ref, aggregate_ref, neighbors_ref, mask_ref, sems,
):
    blocks, slots, size, _ = stiffness_ref.shape
    entries = total_ref.shape[0]
    ghosts = (entries - blocks) // 2
    copies = start_copies([
        (neighbors_hbm, neighbors_ref), (mask_hbm, mask_ref), (aggregate_hbm, aggregate_ref)
    ], sems)
    for copy in copies:
        copy.wait()
    odd = parity()
    peak = jnp.zeros((8, size), f32)
    for b in range(blocks):
        total_ref[...] = jnp.zeros_like(total_ref)
        ratio = jnp.zeros((size, size), f32)
        for s in range(slots):
            entry = neighbors_ref[b, s]
            swapped = jnp.where(entry < blocks + ghosts, entry + ghosts, entry - ghosts)
            entry = jnp.where((entry >= blocks) & (odd == 0), swapped, entry)
            live = stiffness_ref[b, s] * mask_ref[b, s].astype(f32)
            ratio = ratio + jnp.abs(live)
            total_ref[entry] = total_ref[entry] + live.T
        for entry in range(entries):
            parts_ref[b, entry * size : (entry + 1) * size, :] = beside(total_ref[entry])
        rows = lax.dot_general(
            jnp.ones((8, size), f32), ratio, TRANSPOSED,
            precision=lax.Precision.HIGHEST, preferred_element_type=f32,
        )
        peak = jnp.maximum(peak, rows / diagonal_ref[b : b + 1, :])
    peak_ref[...] = jnp.broadcast_to(jnp.max(peak, axis=1, keepdims=True), peak.shape)
    index = lax.broadcasted_iota(jnp.int32, (places_ref.shape[0], size), 0)
    for b in range(blocks):
        hit = index == aggregate_ref[b : b + 1, :]
        places_ref[:, b * size : (b + 1) * size] = hit.astype(f32).astype(bf16)


def couple(field_ref, near_ref, far_ref, parts_ref, diagonal_ref, next_ref):
    blocks, comps, size = field_ref.shape
    ghosts = near_ref.shape[0] // comps
    me = lax.axis_index("wide")
    inside = jnp.where((me == 0) | (me == lax.axis_size("wide") - 1), 0.0, 1.0).astype(f32)
    extended = [stacked(field_ref[b]) for b in range(blocks)]
    extended += [stacked(near_ref[j * comps : (j + 1) * comps]) for j in range(ghosts)]
    extended += [stacked(far_ref[j * comps : (j + 1) * comps] * inside) for j in range(ghosts)]
    extended = jnp.concatenate(extended, axis=1)
    for b in range(blocks):
        product = jnp.dot(extended, parts_ref[b], preferred_element_type=f32)
        coupled = product[:comps, :size] + product[:comps, size:] + product[comps:, :size]
        next_ref[b] = coupled / diagonal_ref[b : b + 1, :]


def step_kernel(field_ref, near_ref, far_ref, parts_ref, diagonal_ref, choice_ref, next_ref, near_out, far_out):
    couple(field_ref, near_ref, far_ref, parts_ref, diagonal_ref, next_ref)
    write_messages(choice_ref, next_ref, near_out, far_out)


def restrict(fields, diagonal_ref, places_ref):
    blocks, comps, size = fields[0].shape
    values = []
    for b in range(blocks):
        scale = diagonal_ref[b : b + 1, :]
        values.append(jnp.concatenate([stacked(field[b] * scale) for field in fields], axis=0))
    product = lax.dot_general(
        jnp.concatenate(values, axis=1), places_ref[...], TRANSPOSED, preferred_element_type=f32
    )
    return [product[2 * k * comps : (2 * k + 1) * comps] + product[(2 * k + 1) * comps : (2 * k + 2) * comps]
            for k in range(len(fields))]


def restrict_kernel(field0_ref, field1_ref, field2_ref, diagonal_ref, places_ref, sums_ref):
    for k, value in enumerate(restrict([field0_ref, field1_ref, field2_ref], diagonal_ref, places_ref)):
        sums_ref[k] = value


def last_step_kernel(field_ref, near_ref, far_ref, parts_ref, diagonal_ref, places_ref, next_ref, sums_ref):
    couple(field_ref, near_ref, far_ref, parts_ref, diagonal_ref, next_ref)
    (sums_ref[...],) = restrict([next_ref], diagonal_ref, places_ref)


def coefficients(upper):
    half_span = 0.375 * upper
    zero = jnp.zeros_like(upper)
    ratio = 5.0 / 3.0
    before = 0.6

    def applied(d):
        return [d[0]] + [d[k] - d[k - 1] for k in range(1, len(d))] + [-d[-1]]

    def less(a, b):
        a = a + [zero] * (len(b) - len(a))
        return [x - y for x, y in zip(a, b)]

    direction = [1.0 / (0.625 * upper)]
    answer = list(direction)
    remainder = [jnp.ones_like(upper)]
    for _ in range(SWEEPS):
        remainder = less(remainder, applied(direction))
        now = 1.0 / (2.0 * ratio - before)
        longer = direction + [zero]
        direction = [now * before * d + (2.0 * now / half_span) * r for d, r in zip(longer, remainder)]
        answer = [a + d for a, d in zip(answer + [zero], direction)]
        before = now
    return less(remainder, applied(direction)), answer


def largest(peaks_ref):
    return 1.0 + jnp.max(peaks_ref[...], axis=0, keepdims=True)


def outgoing_kernel(early_ref, late_ref, peaks_ref, after_ref, outgoing_ref):
    targets, quarter, four, _ = outgoing_ref.shape
    half = quarter * four
    on_residual, _ = coefficients(largest(peaks_ref))
    sums = sum(c * f for c, f in zip(on_residual, [early_ref[0], early_ref[1], early_ref[2], late_ref[...]]))
    narrow = lax.axis_size("narrow")
    for target in range(targets):
        low = (target // narrow) % 2 * half
        for q in range(quarter):
            outgoing_ref[target, q] = sums[low + four * q : low + four * (q + 1)]


def finish_kernel(field0_ref, field1_ref, field2_ref, field3_ref, diagonal_ref, peaks_ref, residual_ref, answer_ref):
    on_residual, on_answer = coefficients(largest(peaks_ref))
    for b in range(field0_ref.shape[0]):
        fields = [field0_ref[b], field1_ref[b], field2_ref[b], field3_ref[b]]
        residual_ref[b] = diagonal_ref[b : b + 1, :] * sum(c * f for c, f in zip(on_residual, fields))
        answer_ref[b] = sum(c * f for c, f in zip(on_answer, fields))


def inverse_kernel(first_ref, second_ref, aggregate_ref, right_ref, places_ref):
    members, span = places_ref.shape
    blocks, size = aggregate_ref.shape
    unknowns = first_ref.shape[1]
    rank, narrow = lax.axis_index("narrow"), lax.axis_size("narrow")
    rows_each = members // narrow
    rows = jnp.concatenate([first_ref[...], second_ref[...]], axis=0)
    for k in range(unknowns // size):
        right_ref[k * size : (k + 1) * size, :] = beside(rows[:, k * size : (k + 1) * size].T)
    index = lax.broadcasted_iota(jnp.int32, (members, size), 0)
    for b in range(blocks):
        aggregate = aggregate_ref[b : b + 1, :]
        offset = (aggregate // rows_each) ^ rank
        row = gathered_position(offset, narrow) * rows_each + aggregate % rows_each
        places_ref[:, b * size : (b + 1) * size] = (index == row).astype(f32).astype(bf16)


def coarse_kernel(own_ref, other_ref, right_ref, places_ref, answer_ref, correction_ref):
    blocks, comps, size = answer_ref.shape
    members = places_ref.shape[0]
    own, other = own_ref[...], other_ref[...]
    first = parity() == 0
    rhs = jnp.where(first, jnp.concatenate([own, other], axis=0), jnp.concatenate([other, own], axis=0))
    product = jnp.dot(stacked(rhs), right_ref[...], preferred_element_type=f32)
    found = stacked(product[:comps, :members] + product[:comps, members:] + product[comps:, :members])
    spread = jnp.dot(found, places_ref[...], preferred_element_type=f32)
    spread = spread[:comps] + spread[comps:]
    for b in range(blocks):
        correction_ref[b] = answer_ref[b] + spread[:, b * size : (b + 1) * size]


def from_hbm(*arrays):
    return [pltpu.with_memory_space_constraint(array, pltpu.HBM) for array in arrays]


def swap(value, axis, bit):
    return lax.ppermute(value, axis, [(i, i ^ bit) for i in range(lax.axis_size(axis))])


def swap_far(value):
    count = lax.axis_size("wide")
    return lax.ppermute(value, "wide", [(i, (i + 1 if i % 2 else i - 1) % count) for i in range(count)])


def gathered_position(offset, narrow):
    count = narrow.bit_length() - 1
    return sum(((offset >> k) & 1) << (count - 1 - k) for k in range(count))


def shards(loads, diagonal, stiffness, neighbors, slot_mask, send_list, aggregate, coarse_inverse):
    blocks, comps, size = loads.shape
    slots = neighbors.shape[1]
    ghosts = send_list.shape[0] // 2
    entries = blocks + 2 * ghosts
    wide, narrow = lax.axis_size("wide"), lax.axis_size("narrow")
    members = coarse_inverse.shape[0] * narrow
    unknowns = coarse_inverse.shape[1]
    field = like(blocks, comps, size)
    message = like(ghosts * comps, size)

    def call(kernel, in_specs, out_shape, scratch=()):
        return pl.pallas_call(
            kernel, in_specs=in_specs, out_specs=jax.tree.map(lambda _: VMEM, out_shape), out_shape=out_shape,
            scratch_shapes=scratch, compiler_params=LIMIT,
        )

    def halo(near, far):
        far = swap_far(far)
        return swap(near, "wide", 1), far

    field0, near, far, scale, choice, live = call(
        start_kernel, [HBM] * 4,
        (field, message, message, like(blocks, size), like(2 * ghosts * blocks, size), like(*stiffness.shape)),
        [
            pltpu.VMEM(loads.shape, f32), pltpu.SMEM(send_list.shape, jnp.int32), pltpu.SemaphoreType.DMA((4,)),
        ],
    )(*from_hbm(send_list, loads, diagonal, stiffness))
    near, far = halo(near, far)
    parts, places, peak = call(
        prepare_kernel, [HBM] * 3 + [VMEM] * 2,
        (
            like(blocks, entries * size, 2 * size, dtype=bf16), like(members, blocks * size, dtype=bf16), like(8, size),
        ),
        [
            pltpu.VMEM((entries, size, size), f32), pltpu.VMEM(aggregate.shape, jnp.int32),
            pltpu.SMEM(neighbors.shape, jnp.int32), pltpu.SMEM(slot_mask.shape, jnp.int32),
            pltpu.SemaphoreType.DMA((3,)),
        ],
    )(*from_hbm(neighbors, slot_mask, aggregate), live, scale)
    step = call(step_kernel, [VMEM] * 6, (field, message, message))
    field1, near, far = step(field0, near, far, parts, scale, choice)
    near, far = halo(near, far)
    peaks = lax.all_to_all(jnp.broadcast_to(peak[:1], (wide * narrow, 1, size)), AXES, 0, 0)
    peaks = peaks.reshape(wide * narrow, size)
    field2, near, far = step(field1, near, far, parts, scale, choice)
    near, far = halo(near, far)
    order = [1 << k for k in reversed(range(narrow.bit_length() - 1))]
    arrived = swap(coarse_inverse, "narrow", order[0])
    early = call(restrict_kernel, [VMEM] * 5, like(3, comps, members))(field0, field1, field2, scale, places)
    field3, late = call(last_step_kernel, [VMEM] * 6, (field, like(comps, members)))(
        field2, near, far, parts, scale, places
    )

    half = comps // 2
    outgoing = call(outgoing_kernel, [VMEM] * 4, like(wide * narrow, half // 4, 4, members))(early, late, peaks, arrived)
    incoming = lax.all_to_all(outgoing, AXES, 0, 0)
    residual, answer = call(finish_kernel, [VMEM] * 6, (field, field))(field0, field1, field2, field3, scale, peaks)
    inverse = jnp.concatenate([coarse_inverse, arrived], axis=0)
    for bit in order[1:-1]:
        inverse = jnp.concatenate([inverse, swap(inverse, "narrow", bit)], axis=0)
    right, reads = call(
        inverse_kernel, [VMEM] * 3,
        (like(unknowns, 2 * members, dtype=bf16), like(members, blocks * size, dtype=bf16)),
    )(inverse, swap(inverse, "narrow", order[-1]), aggregate)
    own = incoming.reshape(wide, narrow, half, members).sum(axis=1)
    own = own.transpose(1, 0, 2).reshape(half, wide * members)
    other = swap(own, "wide", 1)
    correction = call(coarse_kernel, [VMEM] * 5, field)(own, other, right, reads, answer)
    return correction, residual


def solution(mesh):
    return jax.shard_map(
        shards,
        mesh=mesh,
        in_specs=(
            P(AXES, None, None),
            P(AXES, None),
            P(AXES, None, None, None),
            P(AXES, None),
            P(AXES, None),
            P(AXES),
            P(AXES, None),
            P(AXES, None),
        ),
        out_specs=(P(AXES, None, None), P(AXES, None, None)),
        check_vma=False,
    )
```

```python
import jax
import jax.numpy as jnp
from jax import lax
from jax.experimental import pallas as pl
from jax.experimental.pallas import tpu as pltpu
from jax.sharding import PartitionSpec as P

SWEEPS = 2
AXES = ("wide", "narrow")

VMEM = pl.BlockSpec(memory_space=pltpu.VMEM)
SMEM = pl.BlockSpec(memory_space=pltpu.SMEM)
HBM = pl.BlockSpec(memory_space=pl.ANY)
LIMIT = pltpu.CompilerParams(vmem_limit_bytes=32 * 1024 * 1024)

f32 = jnp.float32
bf16 = jnp.bfloat16
TRANSPOSED = (((1,), (1,)), ((), ()))


def like(*shape, dtype=f32):
    return jax.ShapeDtypeStruct(shape, dtype)


def split(value):
    high = value.astype(bf16).astype(f32)
    return high, value - high


def stacked(value):
    return jnp.concatenate(split(value), axis=0).astype(bf16)


def beside(value):
    return jnp.concatenate(split(value), axis=1).astype(bf16)


def parity():
    return lax.rem(lax.axis_index("wide"), 2)


def write_messages(choice_ref, field_ref, near_ref, far_ref):
    blocks, comps, _ = field_ref.shape
    ghosts = choice_ref.shape[0] // (2 * blocks)
    for side, ref in enumerate((near_ref, far_ref)):
        for j in range(ghosts):
            row = (side * ghosts + j) * blocks
            ref[j * comps : (j + 1) * comps] = sum(
                choice_ref[row + b : row + b + 1, :] * field_ref[b] for b in range(blocks)
            )
        if ref.shape[0] > ghosts * comps:
            ref[ghosts * comps :] = jnp.zeros((ref.shape[0] - ghosts * comps, ref.shape[1]), f32)


def start_copies(pairs, sems):
    copies = [pltpu.make_async_copy(source, target, sems.at[k]) for k, (source, target) in enumerate(pairs)]
    for copy in copies:
        copy.start()
    return copies


def start_kernel(
    send_hbm, loads_hbm, diagonal_hbm, stiffness_hbm, inverse_hbm,
    field_ref, near_ref, far_ref, diagonal_ref, choice_ref, stiffness_ref, inverse_ref,
    loads_ref, send_ref, sems,
):
    blocks, _, size = loads_ref.shape
    ghosts = send_ref.shape[0] // 2
    copies = start_copies([
        (send_hbm, send_ref), (diagonal_hbm, diagonal_ref), (loads_hbm, loads_ref), (stiffness_hbm, stiffness_ref),
        (inverse_hbm, inverse_ref),
    ], sems)
    for copy in copies[:3]:
        copy.wait()
    odd = parity()
    for j in range(ghosts):
        for b in range(blocks):
            near = jnp.where(send_ref[(1 - odd) * ghosts + j] == b, 1.0, 0.0)
            far = jnp.where(send_ref[odd * ghosts + j] == b, 1.0, 0.0)
            choice_ref[j * blocks + b : j * blocks + b + 1, :] = jnp.full((1, size), near, f32)
            row = (ghosts + j) * blocks + b
            choice_ref[row : row + 1, :] = jnp.full((1, size), far, f32)
    for b in range(blocks):
        field_ref[b] = loads_ref[b] / diagonal_ref[b : b + 1, :]
    write_messages(choice_ref, field_ref, near_ref, far_ref)
    for copy in copies[3:]:
        copy.wait()


def prepare_kernel(
    neighbors_hbm, mask_hbm, aggregate_hbm, stiffness_ref, diagonal_ref, parts_ref, places_ref, peaks_ref,
    total_ref, aggregate_ref, neighbors_ref, mask_ref, sems,
):
    blocks, slots, size, _ = stiffness_ref.shape
    entries = total_ref.shape[0]
    ghosts = (entries - blocks) // 2
    copies = start_copies([
        (neighbors_hbm, neighbors_ref), (mask_hbm, mask_ref), (aggregate_hbm, aggregate_ref)
    ], sems)
    for copy in copies:
        copy.wait()
    odd = parity()
    peak = jnp.zeros((8, size), f32)
    for b in range(blocks):
        total_ref[...] = jnp.zeros_like(total_ref)
        ratio = jnp.zeros((size, size), f32)
        for s in range(slots):
            entry = neighbors_ref[b, s]
            swapped = jnp.where(entry < blocks + ghosts, entry + ghosts, entry - ghosts)
            entry = jnp.where((entry >= blocks) & (odd == 0), swapped, entry)
            live = stiffness_ref[b, s] * mask_ref[b, s].astype(f32)
            ratio = ratio + jnp.abs(live)
            total_ref[entry] = total_ref[entry] + live.T
        for entry in range(entries):
            parts_ref[b, entry * size : (entry + 1) * size, :] = beside(total_ref[entry])
        rows = lax.dot_general(
            jnp.ones((8, size), f32), ratio, TRANSPOSED,
            precision=lax.Precision.HIGHEST, preferred_element_type=f32,
        )
        peak = jnp.maximum(peak, rows / diagonal_ref[b : b + 1, :])
    peak = jnp.max(peak[:1], axis=1, keepdims=True).reshape(1, 1, 1)
    peaks_ref[...] = jnp.broadcast_to(peak, peaks_ref.shape)
    index = lax.broadcasted_iota(jnp.int32, (places_ref.shape[0], size), 0)
    for b in range(blocks):
        hit = index == aggregate_ref[b : b + 1, :]
        places_ref[:, b * size : (b + 1) * size] = hit.astype(f32).astype(bf16)


def couple(field_ref, near_ref, far_ref, parts_ref, diagonal_ref, next_ref):
    blocks, comps, size = field_ref.shape
    ghosts = (parts_ref.shape[1] // size - blocks) // 2
    me = lax.axis_index("wide")
    inside = jnp.where((me == 0) | (me == lax.axis_size("wide") - 1), 0.0, 1.0).astype(f32)
    extended = [stacked(field_ref[b]) for b in range(blocks)]
    extended += [stacked(near_ref[j * comps : (j + 1) * comps]) for j in range(ghosts)]
    extended += [stacked(far_ref[j * comps : (j + 1) * comps] * inside) for j in range(ghosts)]
    extended = jnp.concatenate(extended, axis=1)
    for b in range(blocks):
        product = jnp.dot(extended, parts_ref[b], preferred_element_type=f32)
        coupled = product[:comps, :size] + product[:comps, size:] + product[comps:, :size]
        next_ref[b] = coupled / diagonal_ref[b : b + 1, :]


def step_kernel(field_ref, near_ref, far_ref, parts_ref, diagonal_ref, choice_ref, next_ref, near_out, far_out):
    couple(field_ref, near_ref, far_ref, parts_ref, diagonal_ref, next_ref)
    write_messages(choice_ref, next_ref, near_out, far_out)


def passing_step_kernel(*refs):
    *inputs, later_ref, next_ref, near_out, far_out, later_out = refs
    later_out[...] = later_ref[...]
    step_kernel(*inputs, next_ref, near_out, far_out)


def restrict(fields, diagonal_ref, places_ref):
    blocks, comps, size = fields[0].shape
    values = []
    for b in range(blocks):
        scale = diagonal_ref[b : b + 1, :]
        values.append(jnp.concatenate([stacked(field[b] * scale) for field in fields], axis=0))
    product = lax.dot_general(
        jnp.concatenate(values, axis=1), places_ref[...], TRANSPOSED, preferred_element_type=f32
    )
    return [product[2 * k * comps : (2 * k + 1) * comps] + product[(2 * k + 1) * comps : (2 * k + 2) * comps]
            for k in range(len(fields))]


def restrict_kernel(field0_ref, field1_ref, field2_ref, diagonal_ref, places_ref, sums_ref):
    for k, value in enumerate(restrict([field0_ref, field1_ref, field2_ref], diagonal_ref, places_ref)):
        sums_ref[k] = value


def last_step_kernel(field_ref, near_ref, far_ref, parts_ref, diagonal_ref, places_ref, next_ref, sums_ref):
    couple(field_ref, near_ref, far_ref, parts_ref, diagonal_ref, next_ref)
    (sums_ref[...],) = restrict([next_ref], diagonal_ref, places_ref)


def coefficients(upper):
    half_span = 0.375 * upper
    zero = jnp.zeros_like(upper)
    ratio = 5.0 / 3.0
    before = 0.6

    def applied(d):
        return [d[0]] + [d[k] - d[k - 1] for k in range(1, len(d))] + [-d[-1]]

    def less(a, b):
        a = a + [zero] * (len(b) - len(a))
        return [x - y for x, y in zip(a, b)]

    direction = [1.0 / (0.625 * upper)]
    answer = list(direction)
    remainder = [jnp.ones_like(upper)]
    for _ in range(SWEEPS):
        remainder = less(remainder, applied(direction))
        now = 1.0 / (2.0 * ratio - before)
        longer = direction + [zero]
        direction = [now * before * d + (2.0 * now / half_span) * r for d, r in zip(longer, remainder)]
        answer = [a + d for a, d in zip(answer + [zero], direction)]
        before = now
    return less(remainder, applied(direction)), answer


def largest(peaks_ref):
    return 1.0 + jnp.max(peaks_ref[...], axis=0, keepdims=True)


def outgoing_kernel(early_ref, late_ref, peaks_ref, after_ref, outgoing_ref):
    targets, quarter, four, _ = outgoing_ref.shape
    half = quarter * four
    on_residual, _ = coefficients(largest(peaks_ref))
    sums = sum(c * f for c, f in zip(on_residual, [early_ref[0], early_ref[1], early_ref[2], late_ref[...]]))
    narrow = lax.axis_size("narrow")
    for target in range(targets):
        low = (target // narrow) % 2 * half
        for q in range(quarter):
            outgoing_ref[target, q] = sums[low + four * q : low + four * (q + 1)]


def finish_kernel(field0_ref, field1_ref, field2_ref, field3_ref, diagonal_ref, peaks_ref, residual_ref, answer_ref):
    on_residual, on_answer = coefficients(largest(peaks_ref))
    for b in range(field0_ref.shape[0]):
        fields = [field0_ref[b], field1_ref[b], field2_ref[b], field3_ref[b]]
        residual_ref[b] = diagonal_ref[b : b + 1, :] * sum(c * f for c, f in zip(on_residual, fields))
        answer_ref[b] = sum(c * f for c, f in zip(on_answer, fields))


def inverse_kernel(aggregate_ref, *refs):
    *gathered, right_ref, places_ref = refs
    members = places_ref.shape[0]
    blocks, size = aggregate_ref.shape
    unknowns = right_ref.shape[0]
    rank, narrow = lax.axis_index("narrow"), lax.axis_size("narrow")
    rows_each = members // narrow
    rows = jnp.concatenate([ref[...] for ref in gathered], axis=0)
    for k in range(unknowns // size):
        right_ref[k * size : (k + 1) * size, :] = beside(rows[:, k * size : (k + 1) * size].T)
    index = lax.broadcasted_iota(jnp.int32, (members, size), 0)
    for b in range(blocks):
        aggregate = aggregate_ref[b : b + 1, :]
        offset = (aggregate // rows_each) ^ rank
        row = gathered_position(offset, narrow) * rows_each + aggregate % rows_each
        places_ref[:, b * size : (b + 1) * size] = (index == row).astype(f32).astype(bf16)


def coarse_kernel(own_ref, other_ref, right_ref, places_ref, answer_ref, correction_ref):
    blocks, comps, size = answer_ref.shape
    members = places_ref.shape[0]
    own, other = own_ref[...], other_ref[...]
    first = parity() == 0
    rhs = jnp.where(first, jnp.concatenate([own, other], axis=0), jnp.concatenate([other, own], axis=0))
    product = jnp.dot(stacked(rhs), right_ref[...], preferred_element_type=f32)
    found = stacked(product[:comps, :members] + product[:comps, members:] + product[comps:, :members])
    spread = jnp.dot(found, places_ref[...], preferred_element_type=f32)
    spread = spread[:comps] + spread[comps:]
    for b in range(blocks):
        correction_ref[b] = answer_ref[b] + spread[:, b * size : (b + 1) * size]


def from_hbm(*arrays):
    return [pltpu.with_memory_space_constraint(array, pltpu.HBM) for array in arrays]


def swap(value, axis, bit):
    return lax.ppermute(value, axis, [(i, i ^ bit) for i in range(lax.axis_size(axis))])


def swap_far(value):
    count = lax.axis_size("wide")
    return lax.ppermute(value, "wide", [(i, (i + 1 if i % 2 else i - 1) % count) for i in range(count)])


def gathered_position(offset, narrow):
    half = narrow // 2
    return (offset % half) * 2 + offset // half


def shards(loads, diagonal, stiffness, neighbors, slot_mask, send_list, aggregate, coarse_inverse):
    blocks, comps, size = loads.shape
    slots = neighbors.shape[1]
    ghosts = send_list.shape[0] // 2
    entries = blocks + 2 * ghosts
    wide, narrow = lax.axis_size("wide"), lax.axis_size("narrow")
    members = coarse_inverse.shape[0] * narrow
    unknowns = coarse_inverse.shape[1]
    field = like(blocks, comps, size)
    message = like(ghosts * comps, size)

    def call(kernel, in_specs, out_shape, scratch=()):
        return pl.pallas_call(
            kernel, in_specs=in_specs, out_specs=jax.tree.map(lambda _: VMEM, out_shape), out_shape=out_shape,
            scratch_shapes=scratch, compiler_params=LIMIT,
        )

    def halo(near, far):
        far = swap_far(far)
        return swap(near, "wide", 1), far

    field0, near, far, scale, choice, live, inverse = call(
        start_kernel, [HBM] * 5,
        (
            field, message, message, like(blocks, size), like(2 * ghosts * blocks, size), like(*stiffness.shape),
            like(*coarse_inverse.shape),
        ),
        [
            pltpu.VMEM(loads.shape, f32), pltpu.SMEM(send_list.shape, jnp.int32), pltpu.SemaphoreType.DMA((5,)),
        ],
    )(*from_hbm(send_list, loads, diagonal, stiffness, coarse_inverse))
    near, far = halo(near, far)
    parts, places, peaks = call(
        prepare_kernel, [HBM] * 3 + [VMEM] * 2,
        (
            like(blocks, entries * size, 2 * size, dtype=bf16), like(members, blocks * size, dtype=bf16),
            like(wide * narrow, 2, size),
        ),
        [
            pltpu.VMEM((entries, size, size), f32), pltpu.VMEM(aggregate.shape, jnp.int32),
            pltpu.SMEM(neighbors.shape, jnp.int32), pltpu.SMEM(slot_mask.shape, jnp.int32),
            pltpu.SemaphoreType.DMA((3,)),
        ],
    )(*from_hbm(neighbors, slot_mask, aggregate), live, scale)
    step = call(step_kernel, [VMEM] * 6, (field, message, message))
    field1, near, far = step(field0, near, far, parts, scale, choice)
    near, far = halo(near, far)
    peaks = lax.all_to_all(peaks, AXES, 0, 0)
    peaks = peaks[:, 0]
    longer = like(2 * ghosts * comps, size)
    field2, near, far, inverse = call(passing_step_kernel, [VMEM] * 7, (field, longer, longer, like(*coarse_inverse.shape)))(
        field1, near, far, parts, scale, choice, inverse
    )
    near, far = halo(near, far)
    early = call(restrict_kernel, [VMEM] * 5, like(3, comps, members))(field0, field1, field2, scale, places)
    arrived = swap(inverse, "narrow", narrow // 2)
    field3, late = call(last_step_kernel, [VMEM] * 6, (field, like(comps, members)))(
        field2, near, far, parts, scale, places
    )

    half = comps // 2
    outgoing = call(outgoing_kernel, [VMEM] * 4, like(wide * narrow, half // 4, 4, members))(early, late, peaks, arrived)
    incoming = lax.all_to_all(outgoing, AXES, 0, 0)
    residual, answer = call(finish_kernel, [VMEM] * 6, (field, field))(field0, field1, field2, field3, scale, peaks)
    inverse = jnp.concatenate([inverse, arrived], axis=0)
    gathered = [inverse] + [swap(inverse, "narrow", offset) for offset in range(1, narrow // 2)]
    right, reads = call(
        inverse_kernel, [VMEM] * (1 + len(gathered)),
        (like(unknowns, 2 * members, dtype=bf16), like(members, blocks * size, dtype=bf16)),
    )(aggregate, *gathered)
    own = incoming.reshape(wide, narrow, half, members).sum(axis=1)
    own = own.transpose(1, 0, 2).reshape(half, wide * members)
    other = swap(own, "wide", 1)
    correction = call(coarse_kernel, [VMEM] * 5, field)(own, other, right, reads, answer)
    return correction, residual


def solution(mesh):
    return jax.shard_map(
        shards,
        mesh=mesh,
        in_specs=(
            P(AXES, None, None),
            P(AXES, None),
            P(AXES, None, None, None),
            P(AXES, None),
            P(AXES, None),
            P(AXES),
            P(AXES, None),
            P(AXES, None),
        ),
        out_specs=(P(AXES, None, None), P(AXES, None, None)),
        check_vma=False,
    )
```

```python
import jax
import jax.numpy as jnp
from jax import lax
from jax.experimental import pallas as pl
from jax.experimental.pallas import tpu as pltpu
from jax.sharding import PartitionSpec as P

SWEEPS = 2
AXES = ("wide", "narrow")

VMEM = pl.BlockSpec(memory_space=pltpu.VMEM)
SMEM = pl.BlockSpec(memory_space=pltpu.SMEM)
HBM = pl.BlockSpec(memory_space=pl.ANY)
LIMIT = pltpu.CompilerParams(vmem_limit_bytes=32 * 1024 * 1024)

f32 = jnp.float32
bf16 = jnp.bfloat16
TRANSPOSED = (((1,), (1,)), ((), ()))


def like(*shape, dtype=f32):
    return jax.ShapeDtypeStruct(shape, dtype)


def split(value):
    high = value.astype(bf16).astype(f32)
    return high, value - high


def stacked(value):
    return jnp.concatenate(split(value), axis=0).astype(bf16)


def beside(value):
    return jnp.concatenate(split(value), axis=1).astype(bf16)


def parity():
    return lax.rem(lax.axis_index("wide"), 2)


def write_messages(choice_ref, field_ref, near_ref, far_ref):
    blocks, comps, _ = field_ref.shape
    ghosts = choice_ref.shape[0] // (2 * blocks)
    for side, ref in enumerate((near_ref, far_ref)):
        for j in range(ghosts):
            row = (side * ghosts + j) * blocks
            ref[j * comps : (j + 1) * comps] = sum(
                choice_ref[row + b : row + b + 1, :] * field_ref[b] for b in range(blocks)
            )
        if ref.shape[0] > ghosts * comps:
            ref[ghosts * comps :] = jnp.zeros((ref.shape[0] - ghosts * comps, ref.shape[1]), f32)


def start_copies(pairs, sems):
    copies = [pltpu.make_async_copy(source, target, sems.at[k]) for k, (source, target) in enumerate(pairs)]
    for copy in copies:
        copy.start()
    return copies


def start_kernel(
    send_hbm, loads_hbm, diagonal_hbm,
    field_ref, near_ref, far_ref, diagonal_ref, choice_ref,
    loads_ref, send_ref, sems,
):
    blocks, _, size = loads_ref.shape
    ghosts = send_ref.shape[0] // 2
    copies = start_copies([
        (send_hbm, send_ref), (diagonal_hbm, diagonal_ref), (loads_hbm, loads_ref)
    ], sems)
    for copy in copies:
        copy.wait()
    odd = parity()
    for j in range(ghosts):
        for b in range(blocks):
            near = jnp.where(send_ref[(1 - odd) * ghosts + j] == b, 1.0, 0.0)
            far = jnp.where(send_ref[odd * ghosts + j] == b, 1.0, 0.0)
            choice_ref[j * blocks + b : j * blocks + b + 1, :] = jnp.full((1, size), near, f32)
            row = (ghosts + j) * blocks + b
            choice_ref[row : row + 1, :] = jnp.full((1, size), far, f32)
    for b in range(blocks):
        field_ref[b] = loads_ref[b] / diagonal_ref[b : b + 1, :]
    write_messages(choice_ref, field_ref, near_ref, far_ref)


def prepare_kernel(
    neighbors_hbm, mask_hbm, aggregate_hbm, inverse_hbm, stiffness_hbm, diagonal_ref,
    inner_ref, outer_ref, places_ref, inverse_ref, peaks_hbm,
    total_ref, live_ref, stiffness_ref, aggregate_ref, peaks_ref, neighbors_ref, mask_ref, sems,
):
    blocks, slots, size, _ = stiffness_ref.shape
    entries = total_ref.shape[0]
    ghosts = (entries - blocks) // 2
    inside = blocks + ghosts
    copies = start_copies([
        (neighbors_hbm, neighbors_ref), (mask_hbm, mask_ref),
        *((stiffness_hbm.at[b], stiffness_ref.at[b]) for b in range(blocks)),
        (aggregate_hbm, aggregate_ref), (inverse_hbm, inverse_ref),
    ], sems)
    copies[0].wait()
    copies[1].wait()
    peak = jnp.zeros((1, size), f32)
    for b in range(blocks):
        copies[2 + b].wait()
        ratio = jnp.zeros((size, size), f32)
        for s in range(slots):
            live = (stiffness_ref[b, s] * mask_ref[b, s].astype(f32)).T
            live_ref[b, s] = live
            ratio = ratio + jnp.abs(live)
        peak = jnp.maximum(peak, jnp.sum(ratio, axis=0, keepdims=True) / diagonal_ref[b : b + 1, :])
    peak = jnp.max(peak, axis=1, keepdims=True).reshape(1, 1, 1)
    peaks_ref[...] = jnp.broadcast_to(peak, peaks_ref.shape)
    sent = pltpu.make_async_copy(peaks_ref, peaks_hbm, sems.at[len(copies)])
    sent.start()
    odd = parity()
    for b in range(blocks):
        total_ref[...] = jnp.zeros_like(total_ref)
        for s in range(slots):
            entry = neighbors_ref[b, s]
            swapped = jnp.where(entry < inside, entry + ghosts, entry - ghosts)
            entry = jnp.where((entry >= blocks) & (odd == 0), swapped, entry)
            total_ref[entry] = total_ref[entry] + live_ref[b, s]
        for entry in range(entries):
            part = beside(total_ref[entry])
            if entry < inside:
                inner_ref[b, entry * size : (entry + 1) * size, :] = part
            else:
                outer_ref[b, (entry - inside) * size : (entry - inside + 1) * size, :] = part
    for copy in copies[2 + blocks :]:
        copy.wait()
    index = lax.broadcasted_iota(jnp.int32, (places_ref.shape[0], size), 0)
    for b in range(blocks):
        hit = index == aggregate_ref[b : b + 1, :]
        places_ref[:, b * size : (b + 1) * size] = hit.astype(f32).astype(bf16)
    sent.wait()


def products(fields, parts_ref, out_ref, start_ref=None):
    extended = jnp.concatenate([stacked(field) for field in fields], axis=1)
    blocks, comps, size = out_ref.shape
    for b in range(blocks):
        product = jnp.dot(extended, parts_ref[b], preferred_element_type=f32)
        value = product[:comps, :size] + product[:comps, size:] + product[comps:, :size]
        out_ref[b] = value if start_ref is None else start_ref[b] + value


def inner_kernel(field_ref, near_ref, inner_ref, sum_ref):
    blocks, comps, size = field_ref.shape
    ghosts = inner_ref.shape[1] // size - blocks
    fields = [field_ref[b] for b in range(blocks)] + [near_ref[j * comps : (j + 1) * comps] for j in range(ghosts)]
    products(fields, inner_ref, sum_ref)


def couple(sum_ref, far_ref, outer_ref, diagonal_ref, next_ref):
    blocks, comps, size = sum_ref.shape
    ghosts = outer_ref.shape[1] // size
    me = lax.axis_index("wide")
    inside = jnp.where((me == 0) | (me == lax.axis_size("wide") - 1), 0.0, 1.0).astype(f32)
    products([far_ref[j * comps : (j + 1) * comps] * inside for j in range(ghosts)], outer_ref, next_ref, sum_ref)
    for b in range(blocks):
        next_ref[b] = next_ref[b] / diagonal_ref[b : b + 1, :]


def step_kernel(sum_ref, far_ref, outer_ref, diagonal_ref, choice_ref, next_ref, near_out, far_out):
    couple(sum_ref, far_ref, outer_ref, diagonal_ref, next_ref)
    write_messages(choice_ref, next_ref, near_out, far_out)


def passing_step_kernel(*refs):
    *inputs, later_ref, next_ref, near_out, far_out, later_out = refs
    later_out[...] = later_ref[...]
    step_kernel(*inputs, next_ref, near_out, far_out)


def restrict(fields, diagonal_ref, places_ref):
    blocks, comps, size = fields[0].shape
    values = []
    for b in range(blocks):
        scale = diagonal_ref[b : b + 1, :]
        values.append(jnp.concatenate([stacked(field[b] * scale) for field in fields], axis=0))
    product = lax.dot_general(
        jnp.concatenate(values, axis=1), places_ref[...], TRANSPOSED, preferred_element_type=f32
    )
    return [product[2 * k * comps : (2 * k + 1) * comps] + product[(2 * k + 1) * comps : (2 * k + 2) * comps]
            for k in range(len(fields))]


def restrict_kernel(field0_ref, field1_ref, field2_ref, diagonal_ref, places_ref, sums_ref):
    for k, value in enumerate(restrict([field0_ref, field1_ref, field2_ref], diagonal_ref, places_ref)):
        sums_ref[k] = value


def last_step_kernel(sum_ref, far_ref, outer_ref, diagonal_ref, places_ref, next_ref, sums_ref):
    couple(sum_ref, far_ref, outer_ref, diagonal_ref, next_ref)
    (sums_ref[...],) = restrict([next_ref], diagonal_ref, places_ref)


def coefficients(upper):
    half_span = 0.375 * upper
    zero = jnp.zeros_like(upper)
    ratio = 5.0 / 3.0
    before = 0.6

    def applied(d):
        return [d[0]] + [d[k] - d[k - 1] for k in range(1, len(d))] + [-d[-1]]

    def less(a, b):
        a = a + [zero] * (len(b) - len(a))
        return [x - y for x, y in zip(a, b)]

    direction = [1.0 / (0.625 * upper)]
    answer = list(direction)
    remainder = [jnp.ones_like(upper)]
    for _ in range(SWEEPS):
        remainder = less(remainder, applied(direction))
        now = 1.0 / (2.0 * ratio - before)
        longer = direction + [zero]
        direction = [now * before * d + (2.0 * now / half_span) * r for d, r in zip(longer, remainder)]
        answer = [a + d for a, d in zip(answer + [zero], direction)]
        before = now
    return less(remainder, applied(direction)), answer


def largest(peaks_ref):
    return 1.0 + jnp.max(peaks_ref[...], axis=0)[0:1, 0:128]


def outgoing_kernel(early_ref, late_ref, peaks_ref, after_ref, outgoing_ref):
    targets, quarter, four, _ = outgoing_ref.shape
    half = quarter * four
    on_residual, _ = coefficients(largest(peaks_ref))
    sums = sum(c * f for c, f in zip(on_residual, [early_ref[0], early_ref[1], early_ref[2], late_ref[...]]))
    narrow = lax.axis_size("narrow")
    for target in range(targets):
        low = (target // narrow) % 2 * half
        for q in range(quarter):
            outgoing_ref[target, q] = sums[low + four * q : low + four * (q + 1)]


def finish_kernel(field0_ref, field1_ref, field2_ref, field3_ref, diagonal_ref, peaks_ref, residual_ref, answer_ref):
    on_residual, on_answer = coefficients(largest(peaks_ref))
    for b in range(field0_ref.shape[0]):
        fields = [field0_ref[b], field1_ref[b], field2_ref[b], field3_ref[b]]
        residual_ref[b] = diagonal_ref[b : b + 1, :] * sum(c * f for c, f in zip(on_residual, fields))
        answer_ref[b] = sum(c * f for c, f in zip(on_answer, fields))


def inverse_kernel(aggregate_ref, *refs):
    *gathered, right_ref, places_ref = refs
    members = places_ref.shape[0]
    blocks, size = aggregate_ref.shape
    unknowns = right_ref.shape[0]
    rank, narrow = lax.axis_index("narrow"), lax.axis_size("narrow")
    rows_each = members // narrow
    rows = jnp.concatenate([ref[...] for ref in gathered], axis=0)
    for k in range(unknowns // size):
        right_ref[k * size : (k + 1) * size, :] = beside(rows[:, k * size : (k + 1) * size].T)
    index = lax.broadcasted_iota(jnp.int32, (members, size), 0)
    for b in range(blocks):
        aggregate = aggregate_ref[b : b + 1, :]
        offset = (aggregate // rows_each) ^ rank
        row = gathered_position(offset, narrow) * rows_each + aggregate % rows_each
        places_ref[:, b * size : (b + 1) * size] = (index == row).astype(f32).astype(bf16)


def coarse_kernel(own_ref, other_ref, right_ref, places_ref, answer_ref, correction_ref):
    blocks, comps, size = answer_ref.shape
    members = places_ref.shape[0]
    own, other = own_ref[...], other_ref[...]
    first = parity() == 0
    rhs = jnp.where(first, jnp.concatenate([own, other], axis=0), jnp.concatenate([other, own], axis=0))
    product = jnp.dot(stacked(rhs), right_ref[...], preferred_element_type=f32)
    found = stacked(product[:comps, :members] + product[:comps, members:] + product[comps:, :members])
    spread = jnp.dot(found, places_ref[...], preferred_element_type=f32)
    spread = spread[:comps] + spread[comps:]
    for b in range(blocks):
        correction_ref[b] = answer_ref[b] + spread[:, b * size : (b + 1) * size]


def from_hbm(*arrays):
    return [pltpu.with_memory_space_constraint(array, pltpu.HBM) for array in arrays]


def swap(value, axis, bit):
    return lax.ppermute(value, axis, [(i, i ^ bit) for i in range(lax.axis_size(axis))])


def swap_far(value):
    count = lax.axis_size("wide")
    return lax.ppermute(value, "wide", [(i, (i + 1 if i % 2 else i - 1) % count) for i in range(count)])


def gathered_position(offset, narrow):
    half = narrow // 2
    return (offset % half) * 2 + offset // half


def shards(loads, diagonal, stiffness, neighbors, slot_mask, send_list, aggregate, coarse_inverse):
    blocks, comps, size = loads.shape
    slots = neighbors.shape[1]
    ghosts = send_list.shape[0] // 2
    entries = blocks + 2 * ghosts
    wide, narrow = lax.axis_size("wide"), lax.axis_size("narrow")
    members = coarse_inverse.shape[0] * narrow
    unknowns = coarse_inverse.shape[1]
    field = like(blocks, comps, size)
    message = like(ghosts * comps, size)

    def call(kernel, in_specs, out_shape, scratch=(), out_specs=None):
        return pl.pallas_call(
            kernel, in_specs=in_specs, out_specs=out_specs or jax.tree.map(lambda _: VMEM, out_shape), out_shape=out_shape,
            scratch_shapes=scratch, compiler_params=LIMIT,
        )

    def halo(near, far):
        far = swap_far(far)
        return swap(near, "wide", 1), far

    field0, near, far, scale, choice = call(
        start_kernel, [HBM] * 3,
        (field, message, message, like(blocks, size), like(2 * ghosts * blocks, size)),
        [
            pltpu.VMEM(loads.shape, f32), pltpu.SMEM(send_list.shape, jnp.int32), pltpu.SemaphoreType.DMA((3,)),
        ],
    )(*from_hbm(send_list, loads, diagonal))
    near, far = halo(near, far)
    parts = like(blocks, (blocks + ghosts) * size, 2 * size, dtype=bf16)
    peaks = like(wide * narrow, 1, 192)
    inner, outer, places, inverse, peaks = call(
        prepare_kernel, [HBM] * 5 + [VMEM],
        (
            parts, like(blocks, ghosts * size, 2 * size, dtype=bf16),
            like(members, blocks * size, dtype=bf16), like(*coarse_inverse.shape), peaks,
        ),
        [
            pltpu.VMEM((entries, size, size), f32), pltpu.VMEM(stiffness.shape, f32), pltpu.VMEM(stiffness.shape, f32),
            pltpu.VMEM(aggregate.shape, jnp.int32), pltpu.VMEM(peaks.shape, f32),
            pltpu.SMEM(neighbors.shape, jnp.int32), pltpu.SMEM(slot_mask.shape, jnp.int32),
            pltpu.SemaphoreType.DMA((5 + blocks,)),
        ],
        (VMEM, VMEM, VMEM, VMEM, HBM),
    )(*from_hbm(neighbors, slot_mask, aggregate, coarse_inverse, stiffness), scale)
    within = call(inner_kernel, [VMEM] * 3, field)
    field1, near, far = call(step_kernel, [VMEM] * 5, (field, message, message))(
        within(field0, near, inner), far, outer, scale, choice
    )
    near, far = halo(near, far)
    peaks = lax.all_to_all(peaks, AXES, 0, 0)
    longer = like(ghosts * comps, size)
    field2, near, far, inverse = call(passing_step_kernel, [VMEM] * 6, (field, longer, longer, like(*coarse_inverse.shape)))(
        within(field1, near, inner), far, outer, scale, choice, inverse
    )
    near, far = halo(near, far)
    early = call(restrict_kernel, [VMEM] * 5, like(3, comps, members))(field0, field1, field2, scale, places)
    arrived = swap(inverse, "narrow", narrow // 2)
    field3, late = call(last_step_kernel, [VMEM] * 5, (field, like(comps, members)))(
        within(field2, near, inner), far, outer, scale, places
    )

    half = comps // 2
    outgoing = call(outgoing_kernel, [VMEM] * 4, like(wide * narrow, half // 4, 4, members))(early, late, peaks, arrived)
    incoming = lax.all_to_all(outgoing, AXES, 0, 0)
    residual, answer = call(finish_kernel, [VMEM] * 6, (field, field))(field0, field1, field2, field3, scale, peaks)
    inverse = jnp.concatenate([inverse, arrived], axis=0)
    gathered = [inverse] + [swap(inverse, "narrow", offset) for offset in range(1, narrow // 2)]
    right, reads = call(
        inverse_kernel, [VMEM] * (1 + len(gathered)),
        (like(unknowns, 2 * members, dtype=bf16), like(members, blocks * size, dtype=bf16)),
    )(aggregate, *gathered)
    own = incoming.reshape(wide, narrow, half, members).sum(axis=1)
    own = own.transpose(1, 0, 2).reshape(half, wide * members)
    other = swap(own, "wide", 1)
    correction = call(coarse_kernel, [VMEM] * 5, field)(own, other, right, reads, answer)
    return correction, residual


def solution(mesh):
    return jax.shard_map(
        shards,
        mesh=mesh,
        in_specs=(
            P(AXES, None, None),
            P(AXES, None),
            P(AXES, None, None, None),
            P(AXES, None),
            P(AXES, None),
            P(AXES),
            P(AXES, None),
            P(AXES, None),
        ),
        out_specs=(P(AXES, None, None), P(AXES, None, None)),
        check_vma=False,
    )
```

```python
import jax
import jax.numpy as jnp
from jax import lax
from jax.experimental import pallas as pl
from jax.experimental.pallas import tpu as pltpu
from jax.sharding import PartitionSpec as P

SWEEPS = 2
AXES = ("wide", "narrow")

VMEM = pl.BlockSpec(memory_space=pltpu.VMEM)
SMEM = pl.BlockSpec(memory_space=pltpu.SMEM)
HBM = pl.BlockSpec(memory_space=pl.ANY)
LIMIT = pltpu.CompilerParams(vmem_limit_bytes=32 * 1024 * 1024)

f32 = jnp.float32
bf16 = jnp.bfloat16
TRANSPOSED = (((1,), (1,)), ((), ()))


def like(*shape, dtype=f32):
    return jax.ShapeDtypeStruct(shape, dtype)


def split(value):
    high = value.astype(bf16).astype(f32)
    return high, value - high


def stacked(value):
    return jnp.concatenate(split(value), axis=0).astype(bf16)


def beside(value):
    return jnp.concatenate(split(value), axis=1).astype(bf16)


def parity():
    return lax.rem(lax.axis_index("wide"), 2)


def write_messages(choice_ref, field_ref, near_ref, far_ref):
    blocks, comps, _ = field_ref.shape
    ghosts = choice_ref.shape[0] // (2 * blocks)
    for side, ref in enumerate((near_ref, far_ref)):
        for j in range(ghosts):
            row = (side * ghosts + j) * blocks
            ref[j * comps : (j + 1) * comps] = sum(
                choice_ref[row + b : row + b + 1, :] * field_ref[b] for b in range(blocks)
            )
        if ref.shape[0] > ghosts * comps:
            ref[ghosts * comps :] = jnp.zeros((ref.shape[0] - ghosts * comps, ref.shape[1]), f32)


def start_copies(pairs, sems):
    copies = [pltpu.make_async_copy(source, target, sems.at[k]) for k, (source, target) in enumerate(pairs)]
    for copy in copies:
        copy.start()
    return copies


def start_kernel(
    send_hbm, loads_hbm, diagonal_hbm,
    field_ref, near_ref, far_ref, diagonal_ref, choice_ref,
    loads_ref, send_ref, sems,
):
    blocks, _, size = loads_ref.shape
    ghosts = send_ref.shape[0] // 2
    copies = start_copies([
        (send_hbm, send_ref), (diagonal_hbm, diagonal_ref), (loads_hbm, loads_ref)
    ], sems)
    for copy in copies:
        copy.wait()
    odd = parity()
    for j in range(ghosts):
        for b in range(blocks):
            near = jnp.where(send_ref[(1 - odd) * ghosts + j] == b, 1.0, 0.0)
            far = jnp.where(send_ref[odd * ghosts + j] == b, 1.0, 0.0)
            choice_ref[j * blocks + b : j * blocks + b + 1, :] = jnp.full((1, size), near, f32)
            row = (ghosts + j) * blocks + b
            choice_ref[row : row + 1, :] = jnp.full((1, size), far, f32)
    for b in range(blocks):
        field_ref[b] = loads_ref[b] / diagonal_ref[b : b + 1, :]
    write_messages(choice_ref, field_ref, near_ref, far_ref)


def prepare_kernel(
    neighbors_hbm, mask_hbm, aggregate_hbm, inverse_hbm, stiffness_hbm, diagonal_ref,
    inner_ref, outer_ref, places_ref, inverse_ref, peaks_hbm,
    total_ref, live_ref, stiffness_ref, aggregate_ref, peaks_ref, neighbors_ref, mask_ref, sems,
):
    blocks, slots, size, _ = stiffness_ref.shape
    entries = total_ref.shape[0]
    ghosts = (entries - blocks) // 2
    inside = blocks + ghosts
    copies = start_copies([
        (neighbors_hbm, neighbors_ref), (mask_hbm, mask_ref),
        *((stiffness_hbm.at[b], stiffness_ref.at[b]) for b in range(blocks)),
        (aggregate_hbm, aggregate_ref), (inverse_hbm, inverse_ref),
    ], sems)
    copies[0].wait()
    copies[1].wait()
    peak = jnp.zeros((1, size), f32)
    for b in range(blocks):
        copies[2 + b].wait()
        ratio = jnp.zeros((size, size), f32)
        for s in range(slots):
            live = (stiffness_ref[b, s] * mask_ref[b, s].astype(f32)).T
            live_ref[b, s] = live
            ratio = ratio + jnp.abs(live)
        peak = jnp.maximum(peak, jnp.sum(ratio, axis=0, keepdims=True) / diagonal_ref[b : b + 1, :])
    peak = jnp.max(peak, axis=1, keepdims=True).reshape(1, 1, 1)
    peaks_ref[...] = jnp.broadcast_to(peak, peaks_ref.shape)
    sent = pltpu.make_async_copy(peaks_ref, peaks_hbm, sems.at[len(copies)])
    sent.start()
    odd = parity()
    for b in range(blocks):
        total_ref[...] = jnp.zeros_like(total_ref)
        for s in range(slots):
            entry = neighbors_ref[b, s]
            swapped = jnp.where(entry < inside, entry + ghosts, entry - ghosts)
            entry = jnp.where((entry >= blocks) & (odd == 0), swapped, entry)
            total_ref[entry] = total_ref[entry] + live_ref[b, s]
        for entry in range(entries):
            part = beside(total_ref[entry])
            if entry < inside:
                inner_ref[b, entry * size : (entry + 1) * size, :] = part
            else:
                outer_ref[b, (entry - inside) * size : (entry - inside + 1) * size, :] = part
    for copy in copies[2 + blocks :]:
        copy.wait()
    index = lax.broadcasted_iota(jnp.int32, (places_ref.shape[0], size), 0)
    for b in range(blocks):
        hit = index == aggregate_ref[b : b + 1, :]
        places_ref[:, b * size : (b + 1) * size] = hit.astype(f32).astype(bf16)
    sent.wait()


def products(fields, parts_ref, out_ref, start_ref=None):
    extended = jnp.concatenate([stacked(field) for field in fields], axis=1)
    blocks, comps, size = out_ref.shape
    for b in range(blocks):
        product = jnp.dot(extended, parts_ref[b], preferred_element_type=f32)
        value = product[:comps, :size] + product[:comps, size:] + product[comps:, :size]
        out_ref[b] = value if start_ref is None else start_ref[b] + value


def inner_kernel(field_ref, near_ref, inner_ref, sum_ref):
    blocks, comps, size = field_ref.shape
    ghosts = inner_ref.shape[1] // size - blocks
    fields = [field_ref[b] for b in range(blocks)] + [near_ref[j * comps : (j + 1) * comps] for j in range(ghosts)]
    products(fields, inner_ref, sum_ref)


def couple(sum_ref, far_ref, outer_ref, diagonal_ref, next_ref):
    blocks, comps, size = sum_ref.shape
    ghosts = outer_ref.shape[1] // size
    me = lax.axis_index("wide")
    inside = jnp.where((me == 0) | (me == lax.axis_size("wide") - 1), 0.0, 1.0).astype(f32)
    products([far_ref[j * comps : (j + 1) * comps] * inside for j in range(ghosts)], outer_ref, next_ref, sum_ref)
    for b in range(blocks):
        next_ref[b] = next_ref[b] / diagonal_ref[b : b + 1, :]


def step_kernel(sum_ref, far_ref, outer_ref, diagonal_ref, choice_ref, next_ref, near_out, far_out):
    couple(sum_ref, far_ref, outer_ref, diagonal_ref, next_ref)
    write_messages(choice_ref, next_ref, near_out, far_out)


def passing_step_kernel(*refs):
    *inputs, later_ref, next_ref, near_out, far_out, later_out = refs
    later_out[...] = later_ref[...]
    step_kernel(*inputs, next_ref, near_out, far_out)


def restrict(fields, diagonal_ref, places_ref):
    blocks, comps, size = fields[0].shape
    values = []
    for b in range(blocks):
        scale = diagonal_ref[b : b + 1, :]
        values.append(jnp.concatenate([stacked(field[b] * scale) for field in fields], axis=0))
    product = lax.dot_general(
        jnp.concatenate(values, axis=1), places_ref[...], TRANSPOSED, preferred_element_type=f32
    )
    return [product[2 * k * comps : (2 * k + 1) * comps] + product[(2 * k + 1) * comps : (2 * k + 2) * comps]
            for k in range(len(fields))]


def restrict_kernel(field0_ref, field1_ref, field2_ref, diagonal_ref, places_ref, sums_ref):
    for k, value in enumerate(restrict([field0_ref, field1_ref, field2_ref], diagonal_ref, places_ref)):
        sums_ref[k] = value


def last_step_kernel(sum_ref, far_ref, outer_ref, diagonal_ref, places_ref, next_ref, sums_ref):
    couple(sum_ref, far_ref, outer_ref, diagonal_ref, next_ref)
    (sums_ref[...],) = restrict([next_ref], diagonal_ref, places_ref)


def coefficients(upper):
    half_span = 0.375 * upper
    zero = jnp.zeros_like(upper)
    ratio = 5.0 / 3.0
    before = 0.6

    def applied(d):
        return [d[0]] + [d[k] - d[k - 1] for k in range(1, len(d))] + [-d[-1]]

    def less(a, b):
        a = a + [zero] * (len(b) - len(a))
        return [x - y for x, y in zip(a, b)]

    direction = [1.0 / (0.625 * upper)]
    answer = list(direction)
    remainder = [jnp.ones_like(upper)]
    for _ in range(SWEEPS):
        remainder = less(remainder, applied(direction))
        now = 1.0 / (2.0 * ratio - before)
        longer = direction + [zero]
        direction = [now * before * d + (2.0 * now / half_span) * r for d, r in zip(longer, remainder)]
        answer = [a + d for a, d in zip(answer + [zero], direction)]
        before = now
    return less(remainder, applied(direction)), answer


def largest(peaks_ref, size):
    return 1.0 + jnp.max(peaks_ref[...], axis=0)[0:1, :size]


def outgoing_kernel(early_ref, late_ref, peaks_ref, outgoing_ref):
    targets, quarter, four, _ = outgoing_ref.shape
    half = quarter * four
    on_residual, _ = coefficients(largest(peaks_ref, late_ref.shape[1]))
    sums = sum(c * f for c, f in zip(on_residual, [early_ref[0], early_ref[1], early_ref[2], late_ref[...]]))
    narrow = lax.axis_size("narrow")
    for target in range(targets):
        low = (target // narrow) % 2 * half
        for q in range(quarter):
            outgoing_ref[target, q] = sums[low + four * q : low + four * (q + 1)]


def finish_kernel(field0_ref, field1_ref, field2_ref, field3_ref, diagonal_ref, peaks_ref, residual_ref, answer_ref):
    on_residual, on_answer = coefficients(largest(peaks_ref, diagonal_ref.shape[1]))
    for b in range(field0_ref.shape[0]):
        fields = [field0_ref[b], field1_ref[b], field2_ref[b], field3_ref[b]]
        residual_ref[b] = diagonal_ref[b : b + 1, :] * sum(c * f for c, f in zip(on_residual, fields))
        answer_ref[b] = sum(c * f for c, f in zip(on_answer, fields))


def inverse_kernel(aggregate_ref, *refs):
    *gathered, right_ref, places_ref = refs
    members = places_ref.shape[0]
    blocks, size = aggregate_ref.shape
    unknowns = right_ref.shape[0]
    rank, narrow = lax.axis_index("narrow"), lax.axis_size("narrow")
    rows_each = members // narrow
    rows = jnp.concatenate([ref[...] for ref in gathered], axis=0)
    for k in range(unknowns // size):
        right_ref[k * size : (k + 1) * size, :] = beside(rows[:, k * size : (k + 1) * size].T)
    index = lax.broadcasted_iota(jnp.int32, (members, size), 0)
    for b in range(blocks):
        aggregate = aggregate_ref[b : b + 1, :]
        offset = (aggregate // rows_each) ^ rank
        row = gathered_position(offset, narrow) * rows_each + aggregate % rows_each
        places_ref[:, b * size : (b + 1) * size] = (index == row).astype(f32).astype(bf16)


def coarse_kernel(own_ref, other_ref, right_ref, places_ref, answer_ref, correction_ref):
    blocks, comps, size = answer_ref.shape
    members = places_ref.shape[0]
    own, other = own_ref[...], other_ref[...]
    first = parity() == 0
    rhs = jnp.where(first, jnp.concatenate([own, other], axis=0), jnp.concatenate([other, own], axis=0))
    product = jnp.dot(stacked(rhs), right_ref[...], preferred_element_type=f32)
    found = stacked(product[:comps, :members] + product[:comps, members:] + product[comps:, :members])
    spread = jnp.dot(found, places_ref[...], preferred_element_type=f32)
    spread = spread[:comps] + spread[comps:]
    for b in range(blocks):
        correction_ref[b] = answer_ref[b] + spread[:, b * size : (b + 1) * size]


def from_hbm(*arrays):
    return [pltpu.with_memory_space_constraint(array, pltpu.HBM) for array in arrays]


def longer(value, rows):
    times = -(-rows // value.shape[0])
    return jnp.concatenate([value] * times, axis=0)[:rows]


def swap(value, axis, bit):
    return lax.ppermute(value, axis, [(i, i ^ bit) for i in range(lax.axis_size(axis))])


def swap_far(value):
    count = lax.axis_size("wide")
    return lax.ppermute(value, "wide", [(i, (i + 1 if i % 2 else i - 1) % count) for i in range(count)])


def gathered_position(offset, narrow):
    half = narrow // 2
    return (offset % half) * 2 + offset // half


def shards(loads, diagonal, stiffness, neighbors, slot_mask, send_list, aggregate, coarse_inverse):
    blocks, comps, size = loads.shape
    slots = neighbors.shape[1]
    ghosts = send_list.shape[0] // 2
    entries = blocks + 2 * ghosts
    wide, narrow = lax.axis_size("wide"), lax.axis_size("narrow")
    members = coarse_inverse.shape[0] * narrow
    unknowns = coarse_inverse.shape[1]
    field = like(blocks, comps, size)
    message = like(ghosts * comps, size)
    further = like(ghosts * comps + 8, size)
    furthest = like(3 * ghosts * comps // 2, size)

    def call(kernel, in_specs, out_shape, scratch=(), out_specs=None):
        return pl.pallas_call(
            kernel, in_specs=in_specs, out_specs=out_specs or jax.tree.map(lambda _: VMEM, out_shape), out_shape=out_shape,
            scratch_shapes=scratch, compiler_params=LIMIT,
        )

    def halo(near, far):
        far = swap_far(far)
        return swap(near, "wide", 1), far

    field0, near, far, scale, choice = call(
        start_kernel, [HBM] * 3,
        (field, message, further, like(blocks, size), like(2 * ghosts * blocks, size)),
        [
            pltpu.VMEM(loads.shape, f32), pltpu.SMEM(send_list.shape, jnp.int32), pltpu.SemaphoreType.DMA((3,)),
        ],
    )(*from_hbm(send_list, loads, diagonal))
    near, far = halo(near, far)
    parts = like(blocks, (blocks + ghosts) * size, 2 * size, dtype=bf16)
    peaks = like(wide * narrow, 1, 3 * size // 2)
    inner, outer, places, inverse, peaks = call(
        prepare_kernel, [HBM] * 5 + [VMEM],
        (
            parts, like(blocks, ghosts * size, 2 * size, dtype=bf16),
            like(members, blocks * size, dtype=bf16), like(*coarse_inverse.shape), peaks,
        ),
        [
            pltpu.VMEM((entries, size, size), f32), pltpu.VMEM(stiffness.shape, f32), pltpu.VMEM(stiffness.shape, f32),
            pltpu.VMEM(aggregate.shape, jnp.int32), pltpu.VMEM(peaks.shape, f32),
            pltpu.SMEM(neighbors.shape, jnp.int32), pltpu.SMEM(slot_mask.shape, jnp.int32),
            pltpu.SemaphoreType.DMA((5 + blocks,)),
        ],
        (VMEM, VMEM, VMEM, VMEM, HBM),
    )(*from_hbm(neighbors, slot_mask, aggregate, coarse_inverse, stiffness), scale)
    within = call(inner_kernel, [VMEM] * 3, field)
    field1, near, far = call(step_kernel, [VMEM] * 5, (field, message, further))(
        within(field0, near, inner), far, outer, scale, choice
    )
    near, far = halo(near, far)
    peaks = lax.all_to_all(peaks, AXES, 0, 0)
    field2, near, far, inverse = call(passing_step_kernel, [VMEM] * 6, (field, message, furthest, like(*coarse_inverse.shape)))(
        within(field1, near, inner), far, outer, scale, choice, inverse
    )
    near, far = halo(near, far)
    early = call(restrict_kernel, [VMEM] * 5, like(3, comps, members))(field0, field1, field2, scale, places)
    arrived = swap(longer(inverse, 3 * inverse.shape[0] // 2), "narrow", narrow // 2)[: inverse.shape[0]]
    field3, late = call(last_step_kernel, [VMEM] * 5, (field, like(comps, members)))(
        within(field2, near, inner), far, outer, scale, places
    )

    half = comps // 2
    outgoing = call(outgoing_kernel, [VMEM] * 3, like(wide * narrow, half // 4, 4, members))(early, late, peaks)
    incoming = lax.all_to_all(outgoing, AXES, 0, 0)
    residual, answer = call(finish_kernel, [VMEM] * 6, (field, field))(field0, field1, field2, field3, scale, peaks)
    inverse = jnp.concatenate([inverse, arrived], axis=0)
    gathered = [inverse]
    for offset in range(1, narrow // 2):
        sent = longer(inverse, 9 * inverse.shape[0] // 4) if offset == 1 else inverse
        gathered.append(swap(sent, "narrow", offset)[: inverse.shape[0]])
    right, reads = call(
        inverse_kernel, [VMEM] * (1 + len(gathered)),
        (like(unknowns, 2 * members, dtype=bf16), like(members, blocks * size, dtype=bf16)),
    )(aggregate, *gathered)
    own = incoming.reshape(wide, narrow, half, members).sum(axis=1)
    own = own.transpose(1, 0, 2).reshape(half, wide * members)
    other = swap(own, "wide", 1)
    correction = call(coarse_kernel, [VMEM] * 5, field)(own, other, right, reads, answer)
    return correction, residual


def solution(mesh):
    return jax.shard_map(
        shards,
        mesh=mesh,
        in_specs=(
            P(AXES, None, None),
            P(AXES, None),
            P(AXES, None, None, None),
            P(AXES, None),
            P(AXES, None),
            P(AXES),
            P(AXES, None),
            P(AXES, None),
        ),
        out_specs=(P(AXES, None, None), P(AXES, None, None)),
        check_vma=False,
    )
```

```python
import jax
import jax.numpy as jnp
from jax import lax
from jax.experimental import pallas as pl
from jax.experimental.pallas import tpu as pltpu
from jax.sharding import PartitionSpec as P

SWEEPS = 2
AXES = ("wide", "narrow")

VMEM = pl.BlockSpec(memory_space=pltpu.VMEM)
SMEM = pl.BlockSpec(memory_space=pltpu.SMEM)
HBM = pl.BlockSpec(memory_space=pl.ANY)
LIMIT = pltpu.CompilerParams(vmem_limit_bytes=32 * 1024 * 1024)

f32 = jnp.float32
bf16 = jnp.bfloat16
TRANSPOSED = (((1,), (1,)), ((), ()))


def like(*shape, dtype=f32):
    return jax.ShapeDtypeStruct(shape, dtype)


def split(value):
    high = value.astype(bf16).astype(f32)
    return high, value - high


def stacked(value):
    return jnp.concatenate(split(value), axis=0).astype(bf16)


def beside(value):
    return jnp.concatenate(split(value), axis=1).astype(bf16)


def parity():
    return lax.rem(lax.axis_index("wide"), 2)


def write_messages(choice_ref, field_ref, near_ref, far_ref):
    blocks, comps, _ = field_ref.shape
    ghosts = choice_ref.shape[0] // (2 * blocks)
    for side, ref in enumerate((near_ref, far_ref)):
        for j in range(ghosts):
            row = (side * ghosts + j) * blocks
            ref[j * comps : (j + 1) * comps] = sum(
                choice_ref[row + b : row + b + 1, :] * field_ref[b] for b in range(blocks)
            )
        if ref.shape[0] > ghosts * comps:
            ref[ghosts * comps :] = jnp.zeros((ref.shape[0] - ghosts * comps, ref.shape[1]), f32)


def start_copies(pairs, sems):
    copies = [pltpu.make_async_copy(source, target, sems.at[k]) for k, (source, target) in enumerate(pairs)]
    for copy in copies:
        copy.start()
    return copies


def start_kernel(
    send_hbm, loads_hbm, diagonal_hbm, mask_hbm, stiffness_hbm,
    field_ref, near_ref, far_ref, diagonal_ref, choice_ref, live_ref, stiffness_ref,
    loads_ref, send_ref, mask_ref, sems,
):
    blocks, _, size = loads_ref.shape
    ghosts = send_ref.shape[0] // 2
    copies = start_copies([
        (send_hbm, send_ref), (diagonal_hbm, diagonal_ref), (loads_hbm, loads_ref), (mask_hbm, mask_ref),
        (stiffness_hbm, stiffness_ref),
    ], sems)
    for copy in copies[:4]:
        copy.wait()
    odd = parity()
    for j in range(ghosts):
        for b in range(blocks):
            near = jnp.where(send_ref[(1 - odd) * ghosts + j] == b, 1.0, 0.0)
            far = jnp.where(send_ref[odd * ghosts + j] == b, 1.0, 0.0)
            choice_ref[j * blocks + b : j * blocks + b + 1, :] = jnp.full((1, size), near, f32)
            row = (ghosts + j) * blocks + b
            choice_ref[row : row + 1, :] = jnp.full((1, size), far, f32)
    for b in range(blocks):
        field_ref[b] = loads_ref[b] / diagonal_ref[b : b + 1, :]
    write_messages(choice_ref, field_ref, near_ref, far_ref)
    slots = mask_ref.shape[1]
    for b in range(blocks):
        for s in range(slots):
            row = b * slots + s
            live_ref[row : row + 1, :] = jnp.full((1, size), mask_ref[b, s].astype(f32), f32)
    copies[4].wait()


def prepare_kernel(
    neighbors_hbm, aggregate_hbm, inverse_hbm, stiffness_ref, live_ref, diagonal_ref,
    inner_ref, outer_ref, places_ref, inverse_ref, peaks_hbm,
    total_ref, turned_ref, aggregate_ref, peaks_ref, neighbors_ref, sems,
):
    blocks, slots, size, _ = stiffness_ref.shape
    entries = total_ref.shape[0]
    ghosts = (entries - blocks) // 2
    inside = blocks + ghosts
    copies = start_copies([
        (neighbors_hbm, neighbors_ref), (aggregate_hbm, aggregate_ref), (inverse_hbm, inverse_ref)
    ], sems)
    peak = jnp.zeros((1, size), f32)
    for b in range(blocks):
        ratio = jnp.zeros((size, size), f32)
        for s in range(slots):
            row = b * slots + s
            turned = (stiffness_ref[b, s] * live_ref[row : row + 1, :]).T
            turned_ref[b, s] = turned
            ratio = ratio + jnp.abs(turned)
        peak = jnp.maximum(peak, jnp.sum(ratio, axis=0, keepdims=True) / diagonal_ref[b : b + 1, :])
    peak = jnp.max(peak, axis=1, keepdims=True).reshape(1, 1, 1)
    peaks_ref[...] = jnp.broadcast_to(peak, peaks_ref.shape)
    sent = pltpu.make_async_copy(peaks_ref, peaks_hbm, sems.at[len(copies)])
    sent.start()
    copies[0].wait()
    odd = parity()
    for b in range(blocks):
        total_ref[...] = jnp.zeros_like(total_ref)
        for s in range(slots):
            entry = neighbors_ref[b, s]
            swapped = jnp.where(entry < inside, entry + ghosts, entry - ghosts)
            entry = jnp.where((entry >= blocks) & (odd == 0), swapped, entry)
            total_ref[entry] = total_ref[entry] + turned_ref[b, s]
        for entry in range(entries):
            part = beside(total_ref[entry])
            if entry < inside:
                inner_ref[b, entry * size : (entry + 1) * size, :] = part
            else:
                outer_ref[b, (entry - inside) * size : (entry - inside + 1) * size, :] = part
    for copy in copies[1:]:
        copy.wait()
    index = lax.broadcasted_iota(jnp.int32, (places_ref.shape[0], size), 0)
    for b in range(blocks):
        hit = index == aggregate_ref[b : b + 1, :]
        places_ref[:, b * size : (b + 1) * size] = hit.astype(f32).astype(bf16)
    sent.wait()


def products(fields, parts_ref, out_ref, start_ref=None):
    extended = jnp.concatenate([stacked(field) for field in fields], axis=1)
    blocks, comps, size = out_ref.shape
    for b in range(blocks):
        product = jnp.dot(extended, parts_ref[b], preferred_element_type=f32)
        value = product[:comps, :size] + product[:comps, size:] + product[comps:, :size]
        out_ref[b] = value if start_ref is None else start_ref[b] + value


def inner_kernel(field_ref, near_ref, inner_ref, sum_ref):
    blocks, comps, size = field_ref.shape
    ghosts = inner_ref.shape[1] // size - blocks
    fields = [field_ref[b] for b in range(blocks)] + [near_ref[j * comps : (j + 1) * comps] for j in range(ghosts)]
    products(fields, inner_ref, sum_ref)


def couple(sum_ref, far_ref, outer_ref, diagonal_ref, next_ref):
    blocks, comps, size = sum_ref.shape
    ghosts = outer_ref.shape[1] // size
    me = lax.axis_index("wide")
    inside = jnp.where((me == 0) | (me == lax.axis_size("wide") - 1), 0.0, 1.0).astype(f32)
    products([far_ref[j * comps : (j + 1) * comps] * inside for j in range(ghosts)], outer_ref, next_ref, sum_ref)
    for b in range(blocks):
        next_ref[b] = next_ref[b] / diagonal_ref[b : b + 1, :]


def step_kernel(sum_ref, far_ref, outer_ref, diagonal_ref, choice_ref, next_ref, near_out, far_out):
    couple(sum_ref, far_ref, outer_ref, diagonal_ref, next_ref)
    write_messages(choice_ref, next_ref, near_out, far_out)


def passing_step_kernel(*refs):
    *inputs, later_ref, next_ref, near_out, far_out, later_out = refs
    later_out[...] = later_ref[...]
    step_kernel(*inputs, next_ref, near_out, far_out)


def restrict(fields, diagonal_ref, places_ref):
    blocks, comps, size = fields[0].shape
    values = []
    for b in range(blocks):
        scale = diagonal_ref[b : b + 1, :]
        values.append(jnp.concatenate([stacked(field[b] * scale) for field in fields], axis=0))
    product = lax.dot_general(
        jnp.concatenate(values, axis=1), places_ref[...], TRANSPOSED, preferred_element_type=f32
    )
    return [product[2 * k * comps : (2 * k + 1) * comps] + product[(2 * k + 1) * comps : (2 * k + 2) * comps]
            for k in range(len(fields))]


def restrict_kernel(field0_ref, field1_ref, field2_ref, diagonal_ref, places_ref, sums_ref):
    for k, value in enumerate(restrict([field0_ref, field1_ref, field2_ref], diagonal_ref, places_ref)):
        sums_ref[k] = value


def last_step_kernel(sum_ref, far_ref, outer_ref, diagonal_ref, places_ref, next_ref, sums_ref):
    couple(sum_ref, far_ref, outer_ref, diagonal_ref, next_ref)
    (sums_ref[...],) = restrict([next_ref], diagonal_ref, places_ref)


def coefficients(upper):
    half_span = 0.375 * upper
    zero = jnp.zeros_like(upper)
    ratio = 5.0 / 3.0
    before = 0.6

    def applied(d):
        return [d[0]] + [d[k] - d[k - 1] for k in range(1, len(d))] + [-d[-1]]

    def less(a, b):
        a = a + [zero] * (len(b) - len(a))
        return [x - y for x, y in zip(a, b)]

    direction = [1.0 / (0.625 * upper)]
    answer = list(direction)
    remainder = [jnp.ones_like(upper)]
    for _ in range(SWEEPS):
        remainder = less(remainder, applied(direction))
        now = 1.0 / (2.0 * ratio - before)
        longer = direction + [zero]
        direction = [now * before * d + (2.0 * now / half_span) * r for d, r in zip(longer, remainder)]
        answer = [a + d for a, d in zip(answer + [zero], direction)]
        before = now
    return less(remainder, applied(direction)), answer


def largest(peaks_ref, size):
    return 1.0 + jnp.max(peaks_ref[...], axis=0)[0:1, :size]


def outgoing_kernel(early_ref, late_ref, peaks_ref, outgoing_ref):
    targets, quarter, four, _ = outgoing_ref.shape
    half = quarter * four
    on_residual, _ = coefficients(largest(peaks_ref, late_ref.shape[1]))
    sums = sum(c * f for c, f in zip(on_residual, [early_ref[0], early_ref[1], early_ref[2], late_ref[...]]))
    narrow = lax.axis_size("narrow")
    for target in range(targets):
        low = (target // narrow) % 2 * half
        for q in range(quarter):
            outgoing_ref[target, q] = sums[low + four * q : low + four * (q + 1)]


def finish_kernel(field0_ref, field1_ref, field2_ref, field3_ref, diagonal_ref, peaks_ref, residual_ref, answer_ref):
    on_residual, on_answer = coefficients(largest(peaks_ref, diagonal_ref.shape[1]))
    for b in range(field0_ref.shape[0]):
        fields = [field0_ref[b], field1_ref[b], field2_ref[b], field3_ref[b]]
        residual_ref[b] = diagonal_ref[b : b + 1, :] * sum(c * f for c, f in zip(on_residual, fields))
        answer_ref[b] = sum(c * f for c, f in zip(on_answer, fields))


def inverse_kernel(aggregate_ref, *refs):
    *gathered, right_ref, places_ref = refs
    members = places_ref.shape[0]
    blocks, size = aggregate_ref.shape
    unknowns = right_ref.shape[0]
    rank, narrow = lax.axis_index("narrow"), lax.axis_size("narrow")
    rows_each = members // narrow
    rows = jnp.concatenate([ref[...] for ref in gathered], axis=0)
    for k in range(unknowns // size):
        right_ref[k * size : (k + 1) * size, :] = beside(rows[:, k * size : (k + 1) * size].T)
    index = lax.broadcasted_iota(jnp.int32, (members, size), 0)
    for b in range(blocks):
        aggregate = aggregate_ref[b : b + 1, :]
        offset = (aggregate // rows_each) ^ rank
        row = gathered_position(offset, narrow) * rows_each + aggregate % rows_each
        places_ref[:, b * size : (b + 1) * size] = (index == row).astype(f32).astype(bf16)


def coarse_kernel(own_ref, other_ref, right_ref, places_ref, answer_ref, correction_ref):
    blocks, comps, size = answer_ref.shape
    members = places_ref.shape[0]
    own, other = own_ref[...], other_ref[...]
    first = parity() == 0
    rhs = jnp.where(first, jnp.concatenate([own, other], axis=0), jnp.concatenate([other, own], axis=0))
    product = jnp.dot(stacked(rhs), right_ref[...], preferred_element_type=f32)
    found = stacked(product[:comps, :members] + product[:comps, members:] + product[comps:, :members])
    spread = jnp.dot(found, places_ref[...], preferred_element_type=f32)
    spread = spread[:comps] + spread[comps:]
    for b in range(blocks):
        correction_ref[b] = answer_ref[b] + spread[:, b * size : (b + 1) * size]


def from_hbm(*arrays):
    return [pltpu.with_memory_space_constraint(array, pltpu.HBM) for array in arrays]


def longer(value, rows):
    times = -(-rows // value.shape[0])
    return jnp.concatenate([value] * times, axis=0)[:rows]


def swap(value, axis, bit):
    return lax.ppermute(value, axis, [(i, i ^ bit) for i in range(lax.axis_size(axis))])


def swap_far(value):
    count = lax.axis_size("wide")
    return lax.ppermute(value, "wide", [(i, (i + 1 if i % 2 else i - 1) % count) for i in range(count)])


def gathered_position(offset, narrow):
    half = narrow // 2
    return (offset % half) * 2 + offset // half


def shards(loads, diagonal, stiffness, neighbors, slot_mask, send_list, aggregate, coarse_inverse):
    blocks, comps, size = loads.shape
    slots = neighbors.shape[1]
    ghosts = send_list.shape[0] // 2
    entries = blocks + 2 * ghosts
    wide, narrow = lax.axis_size("wide"), lax.axis_size("narrow")
    members = coarse_inverse.shape[0] * narrow
    unknowns = coarse_inverse.shape[1]
    field = like(blocks, comps, size)
    message = like(ghosts * comps, size)
    further = like(ghosts * comps + 8, size)
    furthest = like(3 * ghosts * comps // 2, size)

    def call(kernel, in_specs, out_shape, scratch=(), out_specs=None):
        return pl.pallas_call(
            kernel, in_specs=in_specs, out_specs=out_specs or jax.tree.map(lambda _: VMEM, out_shape), out_shape=out_shape,
            scratch_shapes=scratch, compiler_params=LIMIT,
        )

    def halo(near, far):
        far = swap_far(far)
        return swap(near, "wide", 1), far

    field0, near, far, scale, choice, live, matrix = call(
        start_kernel, [HBM] * 5,
        (
            field, message, further, like(blocks, size), like(2 * ghosts * blocks, size), like(blocks * slots, size),
            like(*stiffness.shape),
        ),
        [
            pltpu.VMEM(loads.shape, f32), pltpu.SMEM(send_list.shape, jnp.int32),
            pltpu.SMEM(slot_mask.shape, jnp.int32), pltpu.SemaphoreType.DMA((5,)),
        ],
    )(*from_hbm(send_list, loads, diagonal, slot_mask, stiffness))
    near, far = halo(near, far)
    parts = like(blocks, (blocks + ghosts) * size, 2 * size, dtype=bf16)
    peaks = like(wide * narrow, 1, 3 * size // 2)
    inner, outer, places, inverse, peaks = call(
        prepare_kernel, [HBM] * 3 + [VMEM] * 3,
        (
            parts, like(blocks, ghosts * size, 2 * size, dtype=bf16),
            like(members, blocks * size, dtype=bf16), like(*coarse_inverse.shape), peaks,
        ),
        [
            pltpu.VMEM((entries, size, size), f32), pltpu.VMEM(stiffness.shape, f32),
            pltpu.VMEM(aggregate.shape, jnp.int32), pltpu.VMEM(peaks.shape, f32),
            pltpu.SMEM(neighbors.shape, jnp.int32), pltpu.SemaphoreType.DMA((4,)),
        ],
        (VMEM, VMEM, VMEM, VMEM, HBM),
    )(*from_hbm(neighbors, aggregate, coarse_inverse), matrix, live, scale)
    within = call(inner_kernel, [VMEM] * 3, field)
    field1, near, far = call(step_kernel, [VMEM] * 5, (field, message, further))(
        within(field0, near, inner), far, outer, scale, choice
    )
    near, far = halo(near, far)
    peaks = lax.all_to_all(peaks, AXES, 0, 0)
    field2, near, far, inverse = call(passing_step_kernel, [VMEM] * 6, (field, message, furthest, like(*coarse_inverse.shape)))(
        within(field1, near, inner), far, outer, scale, choice, inverse
    )
    near, far = halo(near, far)
    early = call(restrict_kernel, [VMEM] * 5, like(3, comps, members))(field0, field1, field2, scale, places)
    arrived = swap(longer(inverse, 3 * inverse.shape[0] // 2), "narrow", narrow // 2)[: inverse.shape[0]]
    field3, late = call(last_step_kernel, [VMEM] * 5, (field, like(comps, members)))(
        within(field2, near, inner), far, outer, scale, places
    )

    half = comps // 2
    outgoing = call(outgoing_kernel, [VMEM] * 3, like(wide * narrow, half // 4, 4, members))(early, late, peaks)
    incoming = lax.all_to_all(outgoing, AXES, 0, 0)
    residual, answer = call(finish_kernel, [VMEM] * 6, (field, field))(field0, field1, field2, field3, scale, peaks)
    inverse = jnp.concatenate([inverse, arrived], axis=0)
    gathered = [inverse]
    for offset in range(1, narrow // 2):
        sent = longer(inverse, 9 * inverse.shape[0] // 4) if offset == 1 else inverse
        gathered.append(swap(sent, "narrow", offset)[: inverse.shape[0]])
    right, reads = call(
        inverse_kernel, [VMEM] * (1 + len(gathered)),
        (like(unknowns, 2 * members, dtype=bf16), like(members, blocks * size, dtype=bf16)),
    )(aggregate, *gathered)
    own = incoming.reshape(wide, narrow, half, members).sum(axis=1)
    own = own.transpose(1, 0, 2).reshape(half, wide * members)
    other = swap(own, "wide", 1)
    correction = call(coarse_kernel, [VMEM] * 5, field)(own, other, right, reads, answer)
    return correction, residual


def solution(mesh):
    return jax.shard_map(
        shards,
        mesh=mesh,
        in_specs=(
            P(AXES, None, None),
            P(AXES, None),
            P(AXES, None, None, None),
            P(AXES, None),
            P(AXES, None),
            P(AXES),
            P(AXES, None),
            P(AXES, None),
        ),
        out_specs=(P(AXES, None, None), P(AXES, None, None)),
        check_vma=False,
    )
```

```python
import jax
import jax.numpy as jnp
from jax import lax
from jax.experimental import pallas as pl
from jax.experimental.pallas import tpu as pltpu
from jax.sharding import PartitionSpec as P

SWEEPS = 2
AXES = ("wide", "narrow")

VMEM = pl.BlockSpec(memory_space=pltpu.VMEM)
SMEM = pl.BlockSpec(memory_space=pltpu.SMEM)
HBM = pl.BlockSpec(memory_space=pl.ANY)
LIMIT = pltpu.CompilerParams(vmem_limit_bytes=32 * 1024 * 1024)

f32 = jnp.float32
bf16 = jnp.bfloat16
TRANSPOSED = (((1,), (1,)), ((), ()))


def like(*shape, dtype=f32):
    return jax.ShapeDtypeStruct(shape, dtype)


def split(value):
    high = value.astype(bf16).astype(f32)
    return high, value - high


def stacked(value):
    return jnp.concatenate(split(value), axis=0).astype(bf16)


def beside(value):
    return jnp.concatenate(split(value), axis=1).astype(bf16)


def parity():
    return lax.rem(lax.axis_index("wide"), 2)


def write_messages(choice_ref, field_ref, near_ref, far_ref):
    blocks, comps, _ = field_ref.shape
    ghosts = choice_ref.shape[0] // (2 * blocks)
    for side, ref in enumerate((near_ref, far_ref)):
        for j in range(ghosts):
            row = (side * ghosts + j) * blocks
            ref[j * comps : (j + 1) * comps] = sum(
                choice_ref[row + b : row + b + 1, :] * field_ref[b] for b in range(blocks)
            )
        if ref.shape[0] > ghosts * comps:
            ref[ghosts * comps :] = jnp.zeros((ref.shape[0] - ghosts * comps, ref.shape[1]), f32)


def start_copies(pairs, sems):
    copies = [pltpu.make_async_copy(source, target, sems.at[k]) for k, (source, target) in enumerate(pairs)]
    for copy in copies:
        copy.start()
    return copies


def start_kernel(
    send_hbm, loads_hbm, diagonal_hbm, mask_hbm, stiffness_hbm,
    field_ref, near_ref, far_ref, diagonal_ref, choice_ref, live_ref, stiffness_ref,
    loads_ref, send_ref, mask_ref, sems,
):
    blocks, _, size = loads_ref.shape
    ghosts = send_ref.shape[0] // 2
    copies = start_copies([
        (send_hbm, send_ref), (diagonal_hbm, diagonal_ref), (loads_hbm, loads_ref), (mask_hbm, mask_ref),
        (stiffness_hbm, stiffness_ref),
    ], sems)
    for copy in copies[:4]:
        copy.wait()
    odd = parity()
    for j in range(ghosts):
        for b in range(blocks):
            near = jnp.where(send_ref[(1 - odd) * ghosts + j] == b, 1.0, 0.0)
            far = jnp.where(send_ref[odd * ghosts + j] == b, 1.0, 0.0)
            choice_ref[j * blocks + b : j * blocks + b + 1, :] = jnp.full((1, size), near, f32)
            row = (ghosts + j) * blocks + b
            choice_ref[row : row + 1, :] = jnp.full((1, size), far, f32)
    for b in range(blocks):
        field_ref[b] = loads_ref[b] / diagonal_ref[b : b + 1, :]
    write_messages(choice_ref, field_ref, near_ref, far_ref)
    slots = mask_ref.shape[1]
    for b in range(blocks):
        for s in range(slots):
            row = b * slots + s
            live_ref[row : row + 1, :] = jnp.full((1, size), mask_ref[b, s].astype(f32), f32)
    copies[4].wait()


def prepare_kernel(
    neighbors_hbm, aggregate_hbm, inverse_hbm, stiffness_ref, live_ref, diagonal_ref,
    inner_ref, outer_ref, places_ref, inverse_ref, peaks_hbm,
    total_ref, turned_ref, aggregate_ref, peaks_ref, neighbors_ref, sems,
):
    blocks, slots, size, _ = stiffness_ref.shape
    entries = total_ref.shape[0]
    ghosts = (entries - blocks) // 2
    inside = blocks + ghosts
    copies = start_copies([
        (neighbors_hbm, neighbors_ref), (aggregate_hbm, aggregate_ref), (inverse_hbm, inverse_ref)
    ], sems)
    peak = jnp.zeros((1, size), f32)
    for b in range(blocks):
        ratio = jnp.zeros((size, size), f32)
        for s in range(slots):
            row = b * slots + s
            turned = (stiffness_ref[b, s] * live_ref[row : row + 1, :]).T
            turned_ref[b, s] = turned
            ratio = ratio + jnp.abs(turned)
        peak = jnp.maximum(peak, jnp.sum(ratio, axis=0, keepdims=True) / diagonal_ref[b : b + 1, :])
    peak = jnp.max(peak, axis=1, keepdims=True).reshape(1, 1, 1)
    peaks_ref[...] = jnp.broadcast_to(peak, peaks_ref.shape)
    sent = pltpu.make_async_copy(peaks_ref, peaks_hbm, sems.at[len(copies)])
    sent.start()
    copies[0].wait()
    odd = parity()
    for b in range(blocks):
        total_ref[...] = jnp.zeros_like(total_ref)
        for s in range(slots):
            entry = neighbors_ref[b, s]
            swapped = jnp.where(entry < inside, entry + ghosts, entry - ghosts)
            entry = jnp.where((entry >= blocks) & (odd == 0), swapped, entry)
            total_ref[entry] = total_ref[entry] + turned_ref[b, s]
        for entry in range(entries):
            part = beside(total_ref[entry])
            if entry < inside:
                inner_ref[b, entry * size : (entry + 1) * size, :] = part
            else:
                outer_ref[b, (entry - inside) * size : (entry - inside + 1) * size, :] = part
    for copy in copies[1:]:
        copy.wait()
    index = lax.broadcasted_iota(jnp.int32, (places_ref.shape[0], size), 0)
    for b in range(blocks):
        hit = index == aggregate_ref[b : b + 1, :]
        places_ref[:, b * size : (b + 1) * size] = hit.astype(f32).astype(bf16)
    sent.wait()


def products(fields, parts_ref, out_ref, start_ref=None):
    extended = jnp.concatenate([stacked(field) for field in fields], axis=1)
    blocks, comps, size = out_ref.shape
    for b in range(blocks):
        product = jnp.dot(extended, parts_ref[b], preferred_element_type=f32)
        value = product[:comps, :size] + product[:comps, size:] + product[comps:, :size]
        out_ref[b] = value if start_ref is None else start_ref[b] + value


def inner_kernel(field_ref, near_ref, inner_ref, sum_ref):
    blocks, comps, size = field_ref.shape
    ghosts = inner_ref.shape[1] // size - blocks
    fields = [field_ref[b] for b in range(blocks)] + [near_ref[j * comps : (j + 1) * comps] for j in range(ghosts)]
    products(fields, inner_ref, sum_ref)


def couple(sum_ref, far_ref, outer_ref, diagonal_ref, next_ref):
    blocks, comps, size = sum_ref.shape
    ghosts = outer_ref.shape[1] // size
    me = lax.axis_index("wide")
    inside = jnp.where((me == 0) | (me == lax.axis_size("wide") - 1), 0.0, 1.0).astype(f32)
    products([far_ref[j * comps : (j + 1) * comps] * inside for j in range(ghosts)], outer_ref, next_ref, sum_ref)
    for b in range(blocks):
        next_ref[b] = next_ref[b] / diagonal_ref[b : b + 1, :]


def step_kernel(sum_ref, far_ref, outer_ref, diagonal_ref, choice_ref, next_ref, near_out, far_out):
    couple(sum_ref, far_ref, outer_ref, diagonal_ref, next_ref)
    write_messages(choice_ref, next_ref, near_out, far_out)


def passing_step_kernel(*refs):
    *inputs, later_ref, next_ref, near_out, far_out, later_out = refs
    later_out[...] = later_ref[...]
    step_kernel(*inputs, next_ref, near_out, far_out)


def restrict(fields, diagonal_ref, places_ref):
    blocks, comps, size = fields[0].shape
    values = []
    for b in range(blocks):
        scale = diagonal_ref[b : b + 1, :]
        values.append(jnp.concatenate([stacked(field[b] * scale) for field in fields], axis=0))
    product = lax.dot_general(
        jnp.concatenate(values, axis=1), places_ref[...], TRANSPOSED, preferred_element_type=f32
    )
    return [product[2 * k * comps : (2 * k + 1) * comps] + product[(2 * k + 1) * comps : (2 * k + 2) * comps]
            for k in range(len(fields))]


def restrict_kernel(field0_ref, field1_ref, field2_ref, diagonal_ref, places_ref, sums_ref):
    for k, value in enumerate(restrict([field0_ref, field1_ref, field2_ref], diagonal_ref, places_ref)):
        sums_ref[k] = value


def last_step_kernel(sum_ref, far_ref, outer_ref, diagonal_ref, places_ref, next_ref, sums_ref):
    couple(sum_ref, far_ref, outer_ref, diagonal_ref, next_ref)
    (sums_ref[...],) = restrict([next_ref], diagonal_ref, places_ref)


def coefficients(upper):
    half_span = 0.375 * upper
    zero = jnp.zeros_like(upper)
    ratio = 5.0 / 3.0
    before = 0.6

    def applied(d):
        return [d[0]] + [d[k] - d[k - 1] for k in range(1, len(d))] + [-d[-1]]

    def less(a, b):
        a = a + [zero] * (len(b) - len(a))
        return [x - y for x, y in zip(a, b)]

    direction = [1.0 / (0.625 * upper)]
    answer = list(direction)
    remainder = [jnp.ones_like(upper)]
    for _ in range(SWEEPS):
        remainder = less(remainder, applied(direction))
        now = 1.0 / (2.0 * ratio - before)
        longer = direction + [zero]
        direction = [now * before * d + (2.0 * now / half_span) * r for d, r in zip(longer, remainder)]
        answer = [a + d for a, d in zip(answer + [zero], direction)]
        before = now
    return less(remainder, applied(direction)), answer


def largest(peaks_ref):
    return 1.0 + jnp.max(peaks_ref[...], axis=0)[0:1]


def outgoing_kernel(early_ref, late_ref, peaks_ref, outgoing_ref):
    targets, quarter, four, _ = outgoing_ref.shape
    half = quarter * four
    on_residual, _ = coefficients(largest(peaks_ref))
    sums = sum(c * f for c, f in zip(on_residual, [early_ref[0], early_ref[1], early_ref[2], late_ref[...]]))
    narrow = lax.axis_size("narrow")
    for target in range(targets):
        low = (target // narrow) % 2 * half
        for q in range(quarter):
            outgoing_ref[target, q] = sums[low + four * q : low + four * (q + 1)]


def finish_kernel(field0_ref, field1_ref, field2_ref, field3_ref, diagonal_ref, peaks_ref, residual_ref, answer_ref):
    on_residual, on_answer = coefficients(largest(peaks_ref))
    for b in range(field0_ref.shape[0]):
        fields = [field0_ref[b], field1_ref[b], field2_ref[b], field3_ref[b]]
        residual_ref[b] = diagonal_ref[b : b + 1, :] * sum(c * f for c, f in zip(on_residual, fields))
        answer_ref[b] = sum(c * f for c, f in zip(on_answer, fields))


def inverse_kernel(aggregate_ref, *refs):
    *gathered, right_ref, places_ref = refs
    members = places_ref.shape[0]
    blocks, size = aggregate_ref.shape
    unknowns = right_ref.shape[0]
    rank, narrow = lax.axis_index("narrow"), lax.axis_size("narrow")
    rows_each = members // narrow
    rows = jnp.concatenate([ref[...] for ref in gathered], axis=0)
    for k in range(unknowns // size):
        right_ref[k * size : (k + 1) * size, :] = beside(rows[:, k * size : (k + 1) * size].T)
    index = lax.broadcasted_iota(jnp.int32, (members, size), 0)
    for b in range(blocks):
        aggregate = aggregate_ref[b : b + 1, :]
        offset = (aggregate // rows_each) ^ rank
        row = gathered_position(offset, narrow) * rows_each + aggregate % rows_each
        places_ref[:, b * size : (b + 1) * size] = (index == row).astype(f32).astype(bf16)


def coarse_kernel(own_ref, other_ref, right_ref, places_ref, answer_ref, correction_ref):
    blocks, comps, size = answer_ref.shape
    members = places_ref.shape[0]
    own, other = own_ref[...], other_ref[...]
    first = parity() == 0
    rhs = jnp.where(first, jnp.concatenate([own, other], axis=0), jnp.concatenate([other, own], axis=0))
    product = jnp.dot(stacked(rhs), right_ref[...], preferred_element_type=f32)
    found = stacked(product[:comps, :members] + product[:comps, members:] + product[comps:, :members])
    spread = jnp.dot(found, places_ref[...], preferred_element_type=f32)
    spread = spread[:comps] + spread[comps:]
    for b in range(blocks):
        correction_ref[b] = answer_ref[b] + spread[:, b * size : (b + 1) * size]


def from_hbm(*arrays):
    return [pltpu.with_memory_space_constraint(array, pltpu.HBM) for array in arrays]


def longer(value, rows):
    times = -(-rows // value.shape[0])
    return jnp.concatenate([value] * times, axis=0)[:rows]


def swap(value, axis, bit):
    return lax.ppermute(value, axis, [(i, i ^ bit) for i in range(lax.axis_size(axis))])


def swap_far(value):
    count = lax.axis_size("wide")
    return lax.ppermute(value, "wide", [(i, (i + 1 if i % 2 else i - 1) % count) for i in range(count)])


def gathered_position(offset, narrow):
    half = narrow // 2
    return (offset % half) * 2 + offset // half


def shards(loads, diagonal, stiffness, neighbors, slot_mask, send_list, aggregate, coarse_inverse):
    blocks, comps, size = loads.shape
    slots = neighbors.shape[1]
    ghosts = send_list.shape[0] // 2
    entries = blocks + 2 * ghosts
    wide, narrow = lax.axis_size("wide"), lax.axis_size("narrow")
    members = coarse_inverse.shape[0] * narrow
    unknowns = coarse_inverse.shape[1]
    field = like(blocks, comps, size)
    message = like(ghosts * comps, size)
    further = like(ghosts * comps + 8, size)

    def call(kernel, in_specs, out_shape, scratch=(), out_specs=None):
        return pl.pallas_call(
            kernel, in_specs=in_specs, out_specs=out_specs or jax.tree.map(lambda _: VMEM, out_shape), out_shape=out_shape,
            scratch_shapes=scratch, compiler_params=LIMIT,
        )

    def halo(near, far):
        far = swap_far(far)
        return swap(near, "wide", 1), far

    field0, near, far, scale, choice, live, matrix = call(
        start_kernel, [HBM] * 5,
        (
            field, message, further, like(blocks, size), like(2 * ghosts * blocks, size), like(blocks * slots, size),
            like(*stiffness.shape),
        ),
        [
            pltpu.VMEM(loads.shape, f32), pltpu.SMEM(send_list.shape, jnp.int32),
            pltpu.SMEM(slot_mask.shape, jnp.int32), pltpu.SemaphoreType.DMA((5,)),
        ],
    )(*from_hbm(send_list, loads, diagonal, slot_mask, stiffness))
    near, far = halo(near, far)
    parts = like(blocks, (blocks + ghosts) * size, 2 * size, dtype=bf16)
    peaks = like(wide * narrow, 1, size)
    inner, outer, places, inverse, peaks = call(
        prepare_kernel, [HBM] * 3 + [VMEM] * 3,
        (
            parts, like(blocks, ghosts * size, 2 * size, dtype=bf16),
            like(members, blocks * size, dtype=bf16), like(*coarse_inverse.shape), peaks,
        ),
        [
            pltpu.VMEM((entries, size, size), f32), pltpu.VMEM(stiffness.shape, f32),
            pltpu.VMEM(aggregate.shape, jnp.int32), pltpu.VMEM(peaks.shape, f32),
            pltpu.SMEM(neighbors.shape, jnp.int32), pltpu.SemaphoreType.DMA((4,)),
        ],
        (VMEM, VMEM, VMEM, VMEM, HBM),
    )(*from_hbm(neighbors, aggregate, coarse_inverse), matrix, live, scale)
    within = call(inner_kernel, [VMEM] * 3, field)
    field1, near, far = call(step_kernel, [VMEM] * 5, (field, message, further))(
        within(field0, near, inner), far, outer, scale, choice
    )
    near, far = halo(near, far)
    peaks = lax.all_to_all(peaks, AXES, 0, 0)
    field2, near, far, inverse = call(passing_step_kernel, [VMEM] * 6, (field, message, message, like(*coarse_inverse.shape)))(
        within(field1, near, inner), far, outer, scale, choice, inverse
    )
    near, far = halo(near, far)
    early = call(restrict_kernel, [VMEM] * 5, like(3, comps, members))(field0, field1, field2, scale, places)
    arrived = swap(inverse, "narrow", narrow // 2)
    field3, late = call(last_step_kernel, [VMEM] * 5, (field, like(comps, members)))(
        within(field2, near, inner), far, outer, scale, places
    )

    half = comps // 2
    outgoing = call(outgoing_kernel, [VMEM] * 3, like(wide * narrow, half // 4, 4, members))(early, late, peaks)
    incoming = lax.all_to_all(outgoing, AXES, 0, 0)
    residual, answer = call(finish_kernel, [VMEM] * 6, (field, field))(field0, field1, field2, field3, scale, peaks)
    inverse = jnp.concatenate([inverse, arrived], axis=0)
    gathered = [inverse]
    for offset in range(1, narrow // 2):
        sent = longer(inverse, 9 * inverse.shape[0] // 4) if offset == 1 else inverse
        gathered.append(swap(sent, "narrow", offset)[: inverse.shape[0]])
    right, reads = call(
        inverse_kernel, [VMEM] * (1 + len(gathered)),
        (like(unknowns, 2 * members, dtype=bf16), like(members, blocks * size, dtype=bf16)),
    )(aggregate, *gathered)
    own = incoming.reshape(wide, narrow, half, members).sum(axis=1)
    own = own.transpose(1, 0, 2).reshape(half, wide * members)
    other = swap(own, "wide", 1)
    correction = call(coarse_kernel, [VMEM] * 5, field)(own, other, right, reads, answer)
    return correction, residual


def solution(mesh):
    return jax.shard_map(
        shards,
        mesh=mesh,
        in_specs=(
            P(AXES, None, None),
            P(AXES, None),
            P(AXES, None, None, None),
            P(AXES, None),
            P(AXES, None),
            P(AXES),
            P(AXES, None),
            P(AXES, None),
        ),
        out_specs=(P(AXES, None, None), P(AXES, None, None)),
        check_vma=False,
    )
```

```python
import jax
import jax.numpy as jnp
from jax import lax
from jax.experimental import pallas as pl
from jax.experimental.pallas import tpu as pltpu
from jax.sharding import PartitionSpec as P

SWEEPS = 2
AXES = ("wide", "narrow")

VMEM = pl.BlockSpec(memory_space=pltpu.VMEM)
SMEM = pl.BlockSpec(memory_space=pltpu.SMEM)
HBM = pl.BlockSpec(memory_space=pl.ANY)
LIMIT = pltpu.CompilerParams(vmem_limit_bytes=32 * 1024 * 1024)

f32 = jnp.float32
bf16 = jnp.bfloat16
TRANSPOSED = (((1,), (1,)), ((), ()))


def like(*shape, dtype=f32):
    return jax.ShapeDtypeStruct(shape, dtype)


def split(value):
    high = value.astype(bf16).astype(f32)
    return high, value - high


def stacked(value):
    return jnp.concatenate(split(value), axis=0).astype(bf16)


def beside(value):
    return jnp.concatenate(split(value), axis=1).astype(bf16)


def parity():
    return lax.rem(lax.axis_index("wide"), 2)


def write_messages(choice_ref, field_ref, near_ref, far_ref):
    blocks, comps, _ = field_ref.shape
    ghosts = choice_ref.shape[0] // (2 * blocks)
    for side, ref in enumerate((near_ref, far_ref)):
        for j in range(ghosts):
            row = (side * ghosts + j) * blocks
            ref[j * comps : (j + 1) * comps] = sum(
                choice_ref[row + b : row + b + 1, :] * field_ref[b] for b in range(blocks)
            )
        if ref.shape[0] > ghosts * comps:
            ref[ghosts * comps :] = jnp.zeros((ref.shape[0] - ghosts * comps, ref.shape[1]), f32)


def start_copies(pairs, sems):
    copies = [pltpu.make_async_copy(source, target, sems.at[k]) for k, (source, target) in enumerate(pairs)]
    for copy in copies:
        copy.start()
    return copies


def start_kernel(
    send_hbm, loads_hbm, diagonal_hbm, mask_hbm, stiffness_hbm,
    field_ref, near_ref, far_ref, diagonal_ref, choice_ref, live_ref, stiffness_ref,
    loads_ref, send_ref, mask_ref, sems,
):
    blocks, _, size = loads_ref.shape
    ghosts = send_ref.shape[0] // 2
    copies = start_copies([
        *((stiffness_hbm.at[b], stiffness_ref.at[b]) for b in range(blocks)),
        (send_hbm, send_ref), (diagonal_hbm, diagonal_ref), (loads_hbm, loads_ref), (mask_hbm, mask_ref),
    ], sems)
    for copy in copies[blocks:]:
        copy.wait()
    odd = parity()
    for j in range(ghosts):
        for b in range(blocks):
            near = jnp.where(send_ref[(1 - odd) * ghosts + j] == b, 1.0, 0.0)
            far = jnp.where(send_ref[odd * ghosts + j] == b, 1.0, 0.0)
            choice_ref[j * blocks + b : j * blocks + b + 1, :] = jnp.full((1, size), near, f32)
            row = (ghosts + j) * blocks + b
            choice_ref[row : row + 1, :] = jnp.full((1, size), far, f32)
    for b in range(blocks):
        field_ref[b] = loads_ref[b] / diagonal_ref[b : b + 1, :]
    write_messages(choice_ref, field_ref, near_ref, far_ref)
    slots = mask_ref.shape[1]
    for b in range(blocks):
        for s in range(slots):
            row = b * slots + s
            live_ref[row : row + 1, :] = jnp.full((1, size), mask_ref[b, s].astype(f32), f32)
    for copy in copies[:blocks]:
        copy.wait()


def prepare_kernel(
    neighbors_hbm, aggregate_hbm, inverse_hbm, stiffness_ref, live_ref, diagonal_ref,
    inner_ref, outer_ref, places_ref, inverse_ref, peaks_hbm,
    total_ref, turned_ref, aggregate_ref, peaks_ref, neighbors_ref, sems,
):
    blocks, slots, size, _ = stiffness_ref.shape
    entries = total_ref.shape[0]
    ghosts = (entries - blocks) // 2
    inside = blocks + ghosts
    copies = start_copies([
        (neighbors_hbm, neighbors_ref), (aggregate_hbm, aggregate_ref), (inverse_hbm, inverse_ref)
    ], sems)
    peak = jnp.zeros((1, size), f32)
    for b in range(blocks):
        ratio = jnp.zeros((size, size), f32)
        for s in range(slots):
            row = b * slots + s
            turned = (stiffness_ref[b, s] * live_ref[row : row + 1, :]).T
            turned_ref[b, s] = turned
            ratio = ratio + jnp.abs(turned)
        peak = jnp.maximum(peak, jnp.sum(ratio, axis=0, keepdims=True) / diagonal_ref[b : b + 1, :])
    peak = jnp.max(peak, axis=1, keepdims=True).reshape(1, 1, 1)
    peaks_ref[...] = jnp.broadcast_to(peak, peaks_ref.shape)
    sent = pltpu.make_async_copy(peaks_ref, peaks_hbm, sems.at[len(copies)])
    sent.start()
    copies[0].wait()
    odd = parity()
    for b in range(blocks):
        total_ref[...] = jnp.zeros_like(total_ref)
        for s in range(slots):
            entry = neighbors_ref[b, s]
            swapped = jnp.where(entry < inside, entry + ghosts, entry - ghosts)
            entry = jnp.where((entry >= blocks) & (odd == 0), swapped, entry)
            total_ref[entry] = total_ref[entry] + turned_ref[b, s]
        for entry in range(entries):
            part = beside(total_ref[entry])
            if entry < inside:
                inner_ref[b, entry * size : (entry + 1) * size, :] = part
            else:
                outer_ref[b, (entry - inside) * size : (entry - inside + 1) * size, :] = part
    for copy in copies[1:]:
        copy.wait()
    index = lax.broadcasted_iota(jnp.int32, (places_ref.shape[0], size), 0)
    for b in range(blocks):
        hit = index == aggregate_ref[b : b + 1, :]
        places_ref[:, b * size : (b + 1) * size] = hit.astype(f32).astype(bf16)
    sent.wait()


def products(fields, parts_ref, out_ref, start_ref=None):
    extended = jnp.concatenate([stacked(field) for field in fields], axis=1)
    blocks, comps, size = out_ref.shape
    for b in range(blocks):
        product = jnp.dot(extended, parts_ref[b], preferred_element_type=f32)
        value = product[:comps, :size] + product[:comps, size:] + product[comps:, :size]
        out_ref[b] = value if start_ref is None else start_ref[b] + value


def inner_kernel(field_ref, near_ref, inner_ref, sum_ref):
    blocks, comps, size = field_ref.shape
    ghosts = inner_ref.shape[1] // size - blocks
    fields = [field_ref[b] for b in range(blocks)] + [near_ref[j * comps : (j + 1) * comps] for j in range(ghosts)]
    products(fields, inner_ref, sum_ref)


def couple(sum_ref, far_ref, outer_ref, next_ref):
    blocks, comps, size = sum_ref.shape
    ghosts = outer_ref.shape[1] // size
    me = lax.axis_index("wide")
    inside = jnp.where((me == 0) | (me == lax.axis_size("wide") - 1), 0.0, 1.0).astype(f32)
    products([far_ref[j * comps : (j + 1) * comps] * inside for j in range(ghosts)], outer_ref, next_ref, sum_ref)


def over_diagonal(field_ref, diagonal_ref):
    for b in range(field_ref.shape[0]):
        field_ref[b] = field_ref[b] / diagonal_ref[b : b + 1, :]


def step_kernel(sum_ref, far_ref, outer_ref, diagonal_ref, choice_ref, next_ref, near_out, far_out):
    couple(sum_ref, far_ref, outer_ref, next_ref)
    over_diagonal(next_ref, diagonal_ref)
    write_messages(choice_ref, next_ref, near_out, far_out)


def passing_step_kernel(*refs):
    *inputs, later_ref, next_ref, near_out, far_out, later_out = refs
    later_out[...] = later_ref[...]
    step_kernel(*inputs, next_ref, near_out, far_out)


def restrict(fields, diagonal_ref, places_ref):
    blocks, comps, size = fields[0].shape
    values = []
    for b in range(blocks):
        scale = 1.0 if diagonal_ref is None else diagonal_ref[b : b + 1, :]
        values.append(jnp.concatenate([stacked(field[b] * scale) for field in fields], axis=0))
    product = lax.dot_general(
        jnp.concatenate(values, axis=1), places_ref[...], TRANSPOSED, preferred_element_type=f32
    )
    return [product[2 * k * comps : (2 * k + 1) * comps] + product[(2 * k + 1) * comps : (2 * k + 2) * comps]
            for k in range(len(fields))]


def restrict_kernel(field0_ref, field1_ref, field2_ref, diagonal_ref, places_ref, sums_ref):
    for k, value in enumerate(restrict([field0_ref, field1_ref, field2_ref], diagonal_ref, places_ref)):
        sums_ref[k] = value


def last_step_kernel(sum_ref, far_ref, outer_ref, diagonal_ref, places_ref, next_ref, sums_ref):
    couple(sum_ref, far_ref, outer_ref, next_ref)
    (sums_ref[...],) = restrict([next_ref], None, places_ref)
    over_diagonal(next_ref, diagonal_ref)


def coefficients(upper):
    half_span = 0.375 * upper
    zero = jnp.zeros_like(upper)
    ratio = 5.0 / 3.0
    before = 0.6

    def applied(d):
        return [d[0]] + [d[k] - d[k - 1] for k in range(1, len(d))] + [-d[-1]]

    def less(a, b):
        a = a + [zero] * (len(b) - len(a))
        return [x - y for x, y in zip(a, b)]

    direction = [1.0 / (0.625 * upper)]
    answer = list(direction)
    remainder = [jnp.ones_like(upper)]
    for _ in range(SWEEPS):
        remainder = less(remainder, applied(direction))
        now = 1.0 / (2.0 * ratio - before)
        longer = direction + [zero]
        direction = [now * before * d + (2.0 * now / half_span) * r for d, r in zip(longer, remainder)]
        answer = [a + d for a, d in zip(answer + [zero], direction)]
        before = now
    return less(remainder, applied(direction)), answer


def largest(peaks_ref):
    return 1.0 + jnp.max(peaks_ref[...], axis=0)[0:1]


def outgoing_kernel(early_ref, late_ref, peaks_ref, outgoing_ref):
    targets, quarter, four, _ = outgoing_ref.shape
    half = quarter * four
    on_residual, _ = coefficients(largest(peaks_ref))
    sums = sum(c * f for c, f in zip(on_residual, [early_ref[0], early_ref[1], early_ref[2], late_ref[...]]))
    narrow = lax.axis_size("narrow")
    for target in range(targets):
        low = (target // narrow) % 2 * half
        for q in range(quarter):
            outgoing_ref[target, q] = sums[low + four * q : low + four * (q + 1)]


def finish_kernel(field0_ref, field1_ref, field2_ref, field3_ref, diagonal_ref, peaks_ref, residual_ref, answer_ref):
    on_residual, on_answer = coefficients(largest(peaks_ref))
    for b in range(field0_ref.shape[0]):
        fields = [field0_ref[b], field1_ref[b], field2_ref[b], field3_ref[b]]
        residual_ref[b] = diagonal_ref[b : b + 1, :] * sum(c * f for c, f in zip(on_residual, fields))
        answer_ref[b] = sum(c * f for c, f in zip(on_answer, fields))


def inverse_kernel(aggregate_ref, *refs):
    *gathered, right_ref, places_ref = refs
    members = places_ref.shape[0]
    blocks, size = aggregate_ref.shape
    unknowns = right_ref.shape[0]
    rank, narrow = lax.axis_index("narrow"), lax.axis_size("narrow")
    rows_each = members // narrow
    rows = jnp.concatenate([ref[...] for ref in gathered], axis=0)
    for k in range(unknowns // size):
        right_ref[k * size : (k + 1) * size, :] = beside(rows[:, k * size : (k + 1) * size].T)
    index = lax.broadcasted_iota(jnp.int32, (members, size), 0)
    for b in range(blocks):
        aggregate = aggregate_ref[b : b + 1, :]
        offset = (aggregate // rows_each) ^ rank
        row = gathered_position(offset, narrow) * rows_each + aggregate % rows_each
        places_ref[:, b * size : (b + 1) * size] = (index == row).astype(f32).astype(bf16)


def coarse_kernel(own_ref, other_ref, right_ref, places_ref, answer_ref, correction_ref):
    blocks, comps, size = answer_ref.shape
    members = places_ref.shape[0]
    own, other = own_ref[...], other_ref[...]
    first = parity() == 0
    rhs = jnp.where(first, jnp.concatenate([own, other], axis=0), jnp.concatenate([other, own], axis=0))
    product = jnp.dot(stacked(rhs), right_ref[...], preferred_element_type=f32)
    found = stacked(product[:comps, :members] + product[:comps, members:] + product[comps:, :members])
    spread = jnp.dot(found, places_ref[...], preferred_element_type=f32)
    spread = spread[:comps] + spread[comps:]
    for b in range(blocks):
        correction_ref[b] = answer_ref[b] + spread[:, b * size : (b + 1) * size]


def from_hbm(*arrays):
    return [pltpu.with_memory_space_constraint(array, pltpu.HBM) for array in arrays]


def longer(value, rows):
    times = -(-rows // value.shape[0])
    return jnp.concatenate([value] * times, axis=0)[:rows]


def swap(value, axis, bit):
    return lax.ppermute(value, axis, [(i, i ^ bit) for i in range(lax.axis_size(axis))])


def swap_far(value):
    count = lax.axis_size("wide")
    return lax.ppermute(value, "wide", [(i, (i + 1 if i % 2 else i - 1) % count) for i in range(count)])


def gathered_position(offset, narrow):
    half = narrow // 2
    return (offset % half) * 2 + offset // half


def shards(loads, diagonal, stiffness, neighbors, slot_mask, send_list, aggregate, coarse_inverse):
    blocks, comps, size = loads.shape
    slots = neighbors.shape[1]
    ghosts = send_list.shape[0] // 2
    entries = blocks + 2 * ghosts
    wide, narrow = lax.axis_size("wide"), lax.axis_size("narrow")
    members = coarse_inverse.shape[0] * narrow
    unknowns = coarse_inverse.shape[1]
    field = like(blocks, comps, size)
    message = like(ghosts * comps, size)
    further = like(ghosts * comps + 8, size)

    def call(kernel, in_specs, out_shape, scratch=(), out_specs=None):
        return pl.pallas_call(
            kernel, in_specs=in_specs, out_specs=out_specs or jax.tree.map(lambda _: VMEM, out_shape), out_shape=out_shape,
            scratch_shapes=scratch, compiler_params=LIMIT,
        )

    def halo(near, far):
        far = swap_far(far)
        return swap(near, "wide", 1), far

    field0, near, far, scale, choice, live, matrix = call(
        start_kernel, [HBM] * 5,
        (
            field, message, further, like(blocks, size), like(2 * ghosts * blocks, size), like(blocks * slots, size),
            like(*stiffness.shape),
        ),
        [
            pltpu.VMEM(loads.shape, f32), pltpu.SMEM(send_list.shape, jnp.int32),
            pltpu.SMEM(slot_mask.shape, jnp.int32), pltpu.SemaphoreType.DMA((4 + blocks,)),
        ],
    )(*from_hbm(send_list, loads, diagonal, slot_mask, stiffness))
    near, far = halo(near, far)
    parts = like(blocks, (blocks + ghosts) * size, 2 * size, dtype=bf16)
    peaks = like(wide * narrow, 1, size)
    inner, outer, places, inverse, peaks = call(
        prepare_kernel, [HBM] * 3 + [VMEM] * 3,
        (
            parts, like(blocks, ghosts * size, 2 * size, dtype=bf16),
            like(members, blocks * size, dtype=bf16), like(*coarse_inverse.shape), peaks,
        ),
        [
            pltpu.VMEM((entries, size, size), f32), pltpu.VMEM(stiffness.shape, f32),
            pltpu.VMEM(aggregate.shape, jnp.int32), pltpu.VMEM(peaks.shape, f32),
            pltpu.SMEM(neighbors.shape, jnp.int32), pltpu.SemaphoreType.DMA((4,)),
        ],
        (VMEM, VMEM, VMEM, VMEM, HBM),
    )(*from_hbm(neighbors, aggregate, coarse_inverse), matrix, live, scale)
    within = call(inner_kernel, [VMEM] * 3, field)
    field1, near, far = call(step_kernel, [VMEM] * 5, (field, message, further))(
        within(field0, near, inner), far, outer, scale, choice
    )
    near, far = halo(near, far)
    peaks = lax.all_to_all(peaks, AXES, 0, 0)
    field2, near, far, inverse = call(passing_step_kernel, [VMEM] * 6, (field, message, message, like(*coarse_inverse.shape)))(
        within(field1, near, inner), far, outer, scale, choice, inverse
    )
    near, far = halo(near, far)
    early = call(restrict_kernel, [VMEM] * 5, like(3, comps, members))(field0, field1, field2, scale, places)
    arrived = swap(inverse, "narrow", narrow // 2)
    field3, late = call(last_step_kernel, [VMEM] * 5, (field, like(comps, members)))(
        within(field2, near, inner), far, outer, scale, places
    )

    half = comps // 2
    outgoing = call(outgoing_kernel, [VMEM] * 3, like(wide * narrow, half // 4, 4, members))(early, late, peaks)
    incoming = lax.all_to_all(outgoing, AXES, 0, 0)
    residual, answer = call(finish_kernel, [VMEM] * 6, (field, field))(field0, field1, field2, field3, scale, peaks)
    inverse = jnp.concatenate([inverse, arrived], axis=0)
    gathered = [inverse]
    for offset in range(1, narrow // 2):
        sent = longer(inverse, 9 * inverse.shape[0] // 4) if offset == 1 else inverse
        gathered.append(swap(sent, "narrow", offset)[: inverse.shape[0]])
    right, reads = call(
        inverse_kernel, [VMEM] * (1 + len(gathered)),
        (like(unknowns, 2 * members, dtype=bf16), like(members, blocks * size, dtype=bf16)),
    )(aggregate, *gathered)
    own = incoming.reshape(wide, narrow, half, members).sum(axis=1)
    own = own.transpose(1, 0, 2).reshape(half, wide * members)
    other = swap(own, "wide", 1)
    correction = call(coarse_kernel, [VMEM] * 5, field)(own, other, right, reads, answer)
    return correction, residual


def solution(mesh):
    return jax.shard_map(
        shards,
        mesh=mesh,
        in_specs=(
            P(AXES, None, None),
            P(AXES, None),
            P(AXES, None, None, None),
            P(AXES, None),
            P(AXES, None),
            P(AXES),
            P(AXES, None),
            P(AXES, None),
        ),
        out_specs=(P(AXES, None, None), P(AXES, None, None)),
        check_vma=False,
    )
```

```python
import jax
import jax.numpy as jnp
from jax import lax
from jax.experimental import pallas as pl
from jax.experimental.pallas import tpu as pltpu
from jax.sharding import PartitionSpec as P

SWEEPS = 2
AXES = ("wide", "narrow")

VMEM = pl.BlockSpec(memory_space=pltpu.VMEM)
SMEM = pl.BlockSpec(memory_space=pltpu.SMEM)
HBM = pl.BlockSpec(memory_space=pl.ANY)
LIMIT = pltpu.CompilerParams(vmem_limit_bytes=32 * 1024 * 1024)

f32 = jnp.float32
bf16 = jnp.bfloat16
TRANSPOSED = (((1,), (1,)), ((), ()))


def like(*shape, dtype=f32):
    return jax.ShapeDtypeStruct(shape, dtype)


def split(value):
    high = value.astype(bf16).astype(f32)
    return high, value - high


def stacked(value):
    return jnp.concatenate(split(value), axis=0).astype(bf16)


def beside(value):
    return jnp.concatenate(split(value), axis=1).astype(bf16)


def parity():
    return lax.rem(lax.axis_index("wide"), 2)


def write_messages(choice_ref, field_ref, near_ref, far_ref):
    blocks, comps, _ = field_ref.shape
    ghosts = choice_ref.shape[0] // (2 * blocks)
    for side, ref in enumerate((near_ref, far_ref)):
        for j in range(ghosts):
            row = (side * ghosts + j) * blocks
            ref[j * comps : (j + 1) * comps] = sum(
                choice_ref[row + b : row + b + 1, :] * field_ref[b] for b in range(blocks)
            )
        if ref.shape[0] > ghosts * comps:
            ref[ghosts * comps :] = jnp.zeros((ref.shape[0] - ghosts * comps, ref.shape[1]), f32)


def start_copies(pairs, sems):
    copies = [pltpu.make_async_copy(source, target, sems.at[k]) for k, (source, target) in enumerate(pairs)]
    for copy in copies:
        copy.start()
    return copies


def start_kernel(
    send_hbm, loads_hbm, diagonal_hbm, mask_hbm, stiffness_hbm,
    field_ref, near_ref, far_ref, diagonal_ref, choice_ref, live_ref, stiffness_ref,
    loads_ref, send_ref, mask_ref, sems,
):
    blocks, _, size = loads_ref.shape
    ghosts = send_ref.shape[0] // 2
    copies = start_copies([
        *((stiffness_hbm.at[b], stiffness_ref.at[b]) for b in range(blocks)),
        (send_hbm, send_ref), (diagonal_hbm, diagonal_ref), (loads_hbm, loads_ref), (mask_hbm, mask_ref),
    ], sems)
    for copy in copies[blocks:]:
        copy.wait()
    odd = parity()
    for j in range(ghosts):
        for b in range(blocks):
            near = jnp.where(send_ref[(1 - odd) * ghosts + j] == b, 1.0, 0.0)
            far = jnp.where(send_ref[odd * ghosts + j] == b, 1.0, 0.0)
            choice_ref[j * blocks + b : j * blocks + b + 1, :] = jnp.full((1, size), near, f32)
            row = (ghosts + j) * blocks + b
            choice_ref[row : row + 1, :] = jnp.full((1, size), far, f32)
    for b in range(blocks):
        field_ref[b] = loads_ref[b] / diagonal_ref[b : b + 1, :]
    write_messages(choice_ref, field_ref, near_ref, far_ref)
    slots = mask_ref.shape[1]
    for b in range(blocks):
        for s in range(slots):
            row = b * slots + s
            live_ref[row : row + 1, :] = jnp.full((1, size), mask_ref[b, s].astype(f32), f32)
    for copy in copies[:blocks]:
        copy.wait()


def prepare_kernel(
    neighbors_hbm, aggregate_hbm, inverse_hbm, stiffness_ref, live_ref, diagonal_ref,
    inner_ref, outer_ref, places_ref, inverse_ref, peaks_hbm,
    total_ref, turned_ref, aggregate_ref, peaks_ref, neighbors_ref, sems,
):
    blocks, slots, size, _ = stiffness_ref.shape
    entries = total_ref.shape[0]
    ghosts = (entries - blocks) // 2
    inside = blocks + ghosts
    copies = start_copies([
        (neighbors_hbm, neighbors_ref), (aggregate_hbm, aggregate_ref), (inverse_hbm, inverse_ref)
    ], sems)
    peak = jnp.zeros((1, size), f32)
    for b in range(blocks):
        ratio = jnp.zeros((size, size), f32)
        for s in range(slots):
            row = b * slots + s
            turned = (stiffness_ref[b, s] * live_ref[row : row + 1, :]).T
            turned_ref[b, s] = turned
            ratio = ratio + jnp.abs(turned)
        peak = jnp.maximum(peak, jnp.sum(ratio, axis=0, keepdims=True) / diagonal_ref[b : b + 1, :])
    peak = jnp.max(peak, axis=1, keepdims=True).reshape(1, 1, 1)
    peaks_ref[...] = jnp.broadcast_to(peak, peaks_ref.shape)
    sent = pltpu.make_async_copy(peaks_ref, peaks_hbm, sems.at[len(copies)])
    sent.start()
    copies[0].wait()
    odd = parity()
    for b in range(blocks):
        total_ref[...] = jnp.zeros_like(total_ref)
        for s in range(slots):
            entry = neighbors_ref[b, s]
            swapped = jnp.where(entry < inside, entry + ghosts, entry - ghosts)
            entry = jnp.where((entry >= blocks) & (odd == 0), swapped, entry)
            total_ref[entry] = total_ref[entry] + turned_ref[b, s]
        for entry in range(entries):
            part = beside(total_ref[entry])
            if entry < inside:
                inner_ref[b, entry * size : (entry + 1) * size, :] = part
            else:
                outer_ref[b, (entry - inside) * size : (entry - inside + 1) * size, :] = part
    for copy in copies[1:]:
        copy.wait()
    index = lax.broadcasted_iota(jnp.int32, (places_ref.shape[0], size), 0)
    for b in range(blocks):
        hit = index == aggregate_ref[b : b + 1, :]
        places_ref[:, b * size : (b + 1) * size] = hit.astype(f32).astype(bf16)
    sent.wait()


def products(fields, parts_ref, out_ref, start_ref=None):
    extended = jnp.concatenate([stacked(field) for field in fields], axis=1)
    blocks, comps, size = out_ref.shape
    for b in range(blocks):
        product = jnp.dot(extended, parts_ref[b], preferred_element_type=f32)
        value = product[:comps, :size] + product[:comps, size:] + product[comps:, :size]
        out_ref[b] = value if start_ref is None else start_ref[b] + value


def inner_kernel(field_ref, near_ref, inner_ref, sum_ref):
    blocks, comps, size = field_ref.shape
    ghosts = inner_ref.shape[1] // size - blocks
    fields = [field_ref[b] for b in range(blocks)] + [near_ref[j * comps : (j + 1) * comps] for j in range(ghosts)]
    products(fields, inner_ref, sum_ref)


def couple(sum_ref, far_ref, outer_ref, next_ref):
    blocks, comps, size = sum_ref.shape
    ghosts = outer_ref.shape[1] // size
    me = lax.axis_index("wide")
    inside = jnp.where((me == 0) | (me == lax.axis_size("wide") - 1), 0.0, 1.0).astype(f32)
    products([far_ref[j * comps : (j + 1) * comps] * inside for j in range(ghosts)], outer_ref, next_ref, sum_ref)


def over_diagonal(field_ref, diagonal_ref):
    for b in range(field_ref.shape[0]):
        field_ref[b] = field_ref[b] / diagonal_ref[b : b + 1, :]


def step_kernel(sum_ref, far_ref, outer_ref, diagonal_ref, choice_ref, next_ref, near_out, far_out):
    couple(sum_ref, far_ref, outer_ref, next_ref)
    over_diagonal(next_ref, diagonal_ref)
    write_messages(choice_ref, next_ref, near_out, far_out)


def passing_step_kernel(*refs):
    *inputs, later_ref, next_ref, near_out, far_out, later_out = refs
    later_out[...] = later_ref[...]
    step_kernel(*inputs, next_ref, near_out, far_out)


def restrict(fields, diagonal_ref, places_ref):
    blocks, comps, size = fields[0].shape
    values = []
    for b in range(blocks):
        scale = 1.0 if diagonal_ref is None else diagonal_ref[b : b + 1, :]
        values.append(jnp.concatenate([stacked(field[b] * scale) for field in fields], axis=0))
    product = lax.dot_general(
        jnp.concatenate(values, axis=1), places_ref[...], TRANSPOSED, preferred_element_type=f32
    )
    return [product[2 * k * comps : (2 * k + 1) * comps] + product[(2 * k + 1) * comps : (2 * k + 2) * comps]
            for k in range(len(fields))]


def restrict_kernel(field0_ref, field1_ref, field2_ref, diagonal_ref, places_ref, sums_ref):
    for k, value in enumerate(restrict([field0_ref, field1_ref, field2_ref], diagonal_ref, places_ref)):
        sums_ref[k] = value


def last_step_kernel(sum_ref, far_ref, outer_ref, diagonal_ref, places_ref, next_ref, sums_ref):
    couple(sum_ref, far_ref, outer_ref, next_ref)
    (sums_ref[...],) = restrict([next_ref], None, places_ref)
    over_diagonal(next_ref, diagonal_ref)


def coefficients(upper):
    half_span = 0.375 * upper
    zero = jnp.zeros_like(upper)
    ratio = 5.0 / 3.0
    before = 0.6

    def applied(d):
        return [d[0]] + [d[k] - d[k - 1] for k in range(1, len(d))] + [-d[-1]]

    def less(a, b):
        a = a + [zero] * (len(b) - len(a))
        return [x - y for x, y in zip(a, b)]

    direction = [1.0 / (0.625 * upper)]
    answer = list(direction)
    remainder = [jnp.ones_like(upper)]
    for _ in range(SWEEPS):
        remainder = less(remainder, applied(direction))
        now = 1.0 / (2.0 * ratio - before)
        longer = direction + [zero]
        direction = [now * before * d + (2.0 * now / half_span) * r for d, r in zip(longer, remainder)]
        answer = [a + d for a, d in zip(answer + [zero], direction)]
        before = now
    return less(remainder, applied(direction)), answer


def largest(peaks_ref):
    return 1.0 + jnp.max(peaks_ref[...], axis=0)[0:1]


def outgoing_kernel(early_ref, late_ref, peaks_ref, outgoing_ref):
    targets, quarter, four, _ = outgoing_ref.shape
    half = quarter * four
    on_residual, _ = coefficients(largest(peaks_ref))
    sums = sum(c * f for c, f in zip(on_residual, [early_ref[0], early_ref[1], early_ref[2], late_ref[...]]))
    narrow = lax.axis_size("narrow")
    for target in range(targets):
        low = (target // narrow) % 2 * half
        for q in range(quarter):
            outgoing_ref[target, q] = sums[low + four * q : low + four * (q + 1)]


def finish_kernel(field0_ref, field1_ref, field2_ref, field3_ref, diagonal_ref, peaks_ref, residual_ref, answer_ref):
    on_residual, on_answer = coefficients(largest(peaks_ref))
    for b in range(field0_ref.shape[0]):
        fields = [field0_ref[b], field1_ref[b], field2_ref[b], field3_ref[b]]
        residual_ref[b] = diagonal_ref[b : b + 1, :] * sum(c * f for c, f in zip(on_residual, fields))
        answer_ref[b] = sum(c * f for c, f in zip(on_answer, fields))


def inverse_kernel(aggregate_ref, ahead_ref, *refs):
    *gathered, right_ref, places_ref = refs
    members = places_ref.shape[0]
    blocks, size = aggregate_ref.shape
    unknowns = right_ref.shape[0]
    rank, narrow = lax.axis_index("narrow"), lax.axis_size("narrow")
    rows_each = members // narrow
    rows = jnp.concatenate([ref[...] for ref in gathered], axis=0)
    for k in range(unknowns // size):
        right_ref[k * size : (k + 1) * size, :] = beside(rows[:, k * size : (k + 1) * size].T)
    index = lax.broadcasted_iota(jnp.int32, (members, size), 0)
    for b in range(blocks):
        aggregate = aggregate_ref[b : b + 1, :]
        offset = (aggregate // rows_each) ^ rank
        row = gathered_position(offset, narrow) * rows_each + aggregate % rows_each
        places_ref[:, b * size : (b + 1) * size] = (index == row).astype(f32).astype(bf16)


def coarse_kernel(own_ref, other_ref, right_ref, places_ref, answer_ref, correction_ref):
    blocks, comps, size = answer_ref.shape
    members = places_ref.shape[0]
    own, other = own_ref[...], other_ref[...]
    first = parity() == 0
    rhs = jnp.where(first, jnp.concatenate([own, other], axis=0), jnp.concatenate([other, own], axis=0))
    product = jnp.dot(stacked(rhs), right_ref[...], preferred_element_type=f32)
    found = stacked(product[:comps, :members] + product[:comps, members:] + product[comps:, :members])
    spread = jnp.dot(found, places_ref[...], preferred_element_type=f32)
    spread = spread[:comps] + spread[comps:]
    for b in range(blocks):
        correction_ref[b] = answer_ref[b] + spread[:, b * size : (b + 1) * size]


def from_hbm(*arrays):
    return [pltpu.with_memory_space_constraint(array, pltpu.HBM) for array in arrays]


def longer(value, rows):
    times = -(-rows // value.shape[0])
    return jnp.concatenate([value] * times, axis=0)[:rows]


def swap(value, axis, bit):
    return lax.ppermute(value, axis, [(i, i ^ bit) for i in range(lax.axis_size(axis))])


def swap_far(value):
    count = lax.axis_size("wide")
    return lax.ppermute(value, "wide", [(i, (i + 1 if i % 2 else i - 1) % count) for i in range(count)])


def gathered_position(offset, narrow):
    half = narrow // 2
    return (offset % half) * 2 + offset // half


def shards(loads, diagonal, stiffness, neighbors, slot_mask, send_list, aggregate, coarse_inverse):
    blocks, comps, size = loads.shape
    slots = neighbors.shape[1]
    ghosts = send_list.shape[0] // 2
    entries = blocks + 2 * ghosts
    wide, narrow = lax.axis_size("wide"), lax.axis_size("narrow")
    members = coarse_inverse.shape[0] * narrow
    unknowns = coarse_inverse.shape[1]
    field = like(blocks, comps, size)
    message = like(ghosts * comps, size)
    further = like(ghosts * comps + 8, size)

    def call(kernel, in_specs, out_shape, scratch=(), out_specs=None):
        return pl.pallas_call(
            kernel, in_specs=in_specs, out_specs=out_specs or jax.tree.map(lambda _: VMEM, out_shape), out_shape=out_shape,
            scratch_shapes=scratch, compiler_params=LIMIT,
        )

    def halo(near, far):
        far = swap_far(far)
        return swap(near, "wide", 1), far

    field0, near, far, scale, choice, live, matrix = call(
        start_kernel, [HBM] * 5,
        (
            field, message, further, like(blocks, size), like(2 * ghosts * blocks, size), like(blocks * slots, size),
            like(*stiffness.shape),
        ),
        [
            pltpu.VMEM(loads.shape, f32), pltpu.SMEM(send_list.shape, jnp.int32),
            pltpu.SMEM(slot_mask.shape, jnp.int32), pltpu.SemaphoreType.DMA((4 + blocks,)),
        ],
    )(*from_hbm(send_list, loads, diagonal, slot_mask, stiffness))
    near, far = halo(near, far)
    parts = like(blocks, (blocks + ghosts) * size, 2 * size, dtype=bf16)
    peaks = like(wide * narrow, 1, size)
    inner, outer, places, inverse, peaks = call(
        prepare_kernel, [HBM] * 3 + [VMEM] * 3,
        (
            parts, like(blocks, ghosts * size, 2 * size, dtype=bf16),
            like(members, blocks * size, dtype=bf16), like(*coarse_inverse.shape), peaks,
        ),
        [
            pltpu.VMEM((entries, size, size), f32), pltpu.VMEM(stiffness.shape, f32),
            pltpu.VMEM(aggregate.shape, jnp.int32), pltpu.VMEM(peaks.shape, f32),
            pltpu.SMEM(neighbors.shape, jnp.int32), pltpu.SemaphoreType.DMA((4,)),
        ],
        (VMEM, VMEM, VMEM, VMEM, HBM),
    )(*from_hbm(neighbors, aggregate, coarse_inverse), matrix, live, scale)
    within = call(inner_kernel, [VMEM] * 3, field)
    field1, near, far = call(step_kernel, [VMEM] * 5, (field, message, further))(
        within(field0, near, inner), far, outer, scale, choice
    )
    near, far = halo(near, far)
    peaks = lax.all_to_all(peaks, AXES, 0, 0)
    field2, near, far, inverse = call(passing_step_kernel, [VMEM] * 6, (field, message, message, like(*coarse_inverse.shape)))(
        within(field1, near, inner), far, outer, scale, choice, inverse
    )
    near, far = halo(near, far)
    early = call(restrict_kernel, [VMEM] * 5, like(3, comps, members))(field0, field1, field2, scale, places)
    arrived = swap(inverse, "narrow", narrow // 2)
    field3, late = call(last_step_kernel, [VMEM] * 5, (field, like(comps, members)))(
        within(field2, near, inner), far, outer, scale, places
    )

    half = comps // 2
    outgoing = call(outgoing_kernel, [VMEM] * 3, like(wide * narrow, half // 4, 4, members))(early, late, peaks)
    incoming = lax.all_to_all(outgoing, AXES, 0, 0)
    residual, answer = call(finish_kernel, [VMEM] * 6, (field, field))(field0, field1, field2, field3, scale, peaks)
    inverse = jnp.concatenate([inverse, arrived], axis=0)
    gathered = [inverse] + [swap(inverse, "narrow", offset) for offset in range(1, narrow // 2)]
    ahead = swap(longer(inverse, 9 * inverse.shape[0] // 4), "wide", 1)
    right, reads = call(
        inverse_kernel, [VMEM] * (2 + len(gathered)),
        (like(unknowns, 2 * members, dtype=bf16), like(members, blocks * size, dtype=bf16)),
    )(aggregate, ahead, *gathered)
    own = incoming.reshape(wide, narrow, half, members).sum(axis=1)
    own = own.transpose(1, 0, 2).reshape(half, wide * members)
    other = swap(own, "wide", 1)
    correction = call(coarse_kernel, [VMEM] * 5, field)(own, other, right, reads, answer)
    return correction, residual


def solution(mesh):
    return jax.shard_map(
        shards,
        mesh=mesh,
        in_specs=(
            P(AXES, None, None),
            P(AXES, None),
            P(AXES, None, None, None),
            P(AXES, None),
            P(AXES, None),
            P(AXES),
            P(AXES, None),
            P(AXES, None),
        ),
        out_specs=(P(AXES, None, None), P(AXES, None, None)),
        check_vma=False,
    )
```
